512 devices in a mesh: dp: 16 (over x, y), expert: 32 (over z, core).
Axes of the slice: x: 4, y: 4, z: 16, core: 2. Of those that a mesh axis runs over, the one named last changes fastest.
Arguments:
- tokens: bfloat16 [65536, 2048], P(('dp', 'expert')), may hold values from -6 to 6
- cotangent: bfloat16 [65536, 2048], P(('dp', 'expert')), may hold values from -6 to 6
- routes: int32 [65536, 2], P(('dp', 'expert')), may hold values from 0 to 127, all different within a row; in each aligned block of 128 rows (0 to 127, 128 to 255, ...) at most 3 rows name the same one
- ln_gain: bfloat16 [2048], P('dp'), may hold values from 0.099609375 to 1.8984375
- ln_bias: bfloat16 [2048], P('dp'), may hold values from -3 to 3
- router_weight: bfloat16 [2048, 128], P('dp'), may hold values from -0.25 to 0.25
- up_weight: bfloat16 [32, 256, 8192], P('expert', None, 'dp'), may hold values from -0.125 to 0.125
- down_weight: bfloat16 [32, 8192, 256], P('expert', 'dp'), may hold values from -0.0625 to 0.0625
Outputs:
- moe_out: bfloat16 [65536, 2048], P(('dp', 'expert'))
- grad_input: bfloat16 [65536, 2048], P(('dp', 'expert'))
- grad_up: bfloat16 [32, 256, 8192], P('expert', None, 'dp')
- grad_down: bfloat16 [32, 8192, 256], P('expert', 'dp')
- grad_router: float32 [2048, 128], P('dp')
- grad_gain: float32 [2048], P('dp')
- grad_bias: float32 [2048], P('dp')
The draws below stay inside these ranges and needn't reach their ends.
Inputs may be any that keep to these rules, and one draw needn't show every extreme that they name: `routes`: the two ids of a row differ; the 128 rows of one device name any one expert at most 3 times, a bound that some block reaches.
All inputs are finite; a program needn't handle non-finite values.
Results may differ from the reference program's by a relative error of at most 0.035.
Values may be sent and summed in bfloat16 or wider, within the bound.
A program may use at most 128 MiB of HBM per device.

```python
import math
import jax
import jax.numpy as jnp
import numpy as np
from jax import lax

D = 2048
FF = 8192
ROUTER = 128
TOP = 2
SLICES = 8
TOK_DEV = 128
CAP = 3
DQ = 256
TOKENS = 65536
N_DP = 16
N_EXPERT = 32


def shard_levels(own_key, extent, shards, low, largest):
    def one(dim, blocks):
        steps = jax.random.uniform(jax.random.fold_in(jax.random.fold_in(own_key, 6), dim), (blocks,), jnp.float32, low / len(shards), largest / len(shards))
        return jnp.repeat(jnp.exp(steps), extent[dim] // blocks).reshape((-1,) + (1,) * (len(extent) - dim - 1))

    factor_of = one(*shards[0])
    for cut in shards[1:]:
        factor_of = factor_of * one(*cut)
    return factor_of


def routed_block(stream_key, own, number, rows, amount, top, limit, lean):
    sequence = jax.random.permutation(stream_key, amount)
    heavy_load, common = load_shares(amount, rows * top, limit, lean, True), load_shares(amount, rows * top, limit, lean, False)
    places = jnp.arange(amount)

    def named(tallies, turn):
        used = int((tallies > 0).sum())
        fixed = max(1, used // 4)
        passed = fixed + (places - fixed + turn * (used - fixed)) % max(1, amount - fixed)
        return jnp.zeros((amount,), jnp.int32).at[sequence[jnp.where(places < fixed, places, passed)]].set(jnp.asarray(tallies, jnp.int32))

    tallies = jnp.where(number % 4 == 0, named(heavy_load, number // 4), named(common, number - number // 4 - 1))
    mixed = jax.random.permutation(jax.random.fold_in(own, 3), amount)
    giver, sink = mixed[0:amount // 2 * 2:2], mixed[1:amount // 2 * 2:2]
    room = jnp.minimum(tallies[giver] - 1, limit - tallies[sink]) // 2
    room = jnp.where((giver == sequence[0]) | (sink == sequence[0]) | (tallies[sink] == 0), 0, jnp.maximum(room, 0))
    passed = jax.random.randint(jax.random.fold_in(own, 4), (amount // 2,), 0, 1 << 20) % (room + 1)
    tallies = tallies.at[giver].add(-passed).at[sink].add(passed)
    labels = jnp.searchsorted(jnp.cumsum(tallies), jnp.arange(rows * top), side="right").astype(jnp.int32)
    grid = labels.reshape(top, rows).T
    grid = grid[jax.random.permutation(jax.random.fold_in(own, 1), rows)]
    turn = jax.random.randint(jax.random.fold_in(own, 2), (rows, 1), 0, top)
    return jnp.take_along_axis(grid, (jnp.arange(top)[None, :] + turn) % top, axis=1)


def load_shares(count, total, most, lean, full):
    weights = [(1 << 20) // math.isqrt(grade ** lean) + 1 for grade in range(1, count + 1)]
    largest = most if full else min(most, max(-(-total // count), total * weights[0] // sum(weights)))
    least = 1 if total - largest >= count - 1 else 0
    holding, rest = [largest] + [least] * (count - 1), total - largest - least * (count - 1)
    while rest > 0:
        free = [i for i in range(1, count) if holding[i] < largest] or [i for i in range(1, count) if holding[i] < most]
        mass, budget = sum([weights[i] for i in free]), rest
        for i in free:
            addition = min(most - holding[i], max(1, budget * weights[i] // mass), rest)
            holding[i] = holding[i] + addition
            rest = rest - addition
    return np.array(holding)


def bell_draw(rng, shape, deviation, limit, pieces=(), kind=jnp.bfloat16):
    values = deviation * jax.random.normal(rng, shape, jnp.float32)
    if pieces:
        values = values * shard_levels(rng, shape, pieces, -0.22, 0.18)
    return jnp.clip(values, -limit, limit).astype(kind)


def setup_inputs(seed: int = 0) -> dict:
    splits = jax.random.split(jax.random.key(seed), 9)
    tokens = bell_draw(splits[0], (TOKENS, D), 1.0, 6.0, ((0, 512),))
    cotangent = bell_draw(splits[1], (TOKENS, D), 1.0, 6.0, ((0, 512),))
    routes_keys = jax.random.split(jax.random.fold_in(splits[2], 1), TOKENS // TOK_DEV)
    routes_turns = jax.random.permutation(jax.random.fold_in(splits[2], 3), TOKENS // TOK_DEV)
    routes = jax.vmap(lambda own, number: routed_block(jax.random.fold_in(splits[2], 2), own, number, TOK_DEV, ROUTER, 2, CAP, 2))(routes_keys, routes_turns).reshape((TOKENS, TOP))
    ln_gain = jnp.clip(1.0 + 0.18 * jax.random.normal(splits[3], (D,), jnp.float32), 0.099609375, 1.8984375).astype(jnp.bfloat16)
    ln_bias = bell_draw(splits[4], (D,), 0.5, 3.0, ((0, 16),))
    router_weight = bell_draw(splits[5], (D, ROUTER), (D // 4) ** -0.5, 0.25, ((0, 16),))
    up_weight = bell_draw(splits[6], (N_EXPERT, DQ, FF), D ** -0.5, 0.125, ((0, 32), (2, 16)))
    down_weight = bell_draw(splits[7], (N_EXPERT, FF, DQ), FF ** -0.5, 0.0625, ((0, 32), (1, 16)))
    return {"tokens": tokens, "cotangent": cotangent, "routes": routes, "ln_gain": ln_gain, "ln_bias": ln_bias, "router_weight": router_weight, "up_weight": up_weight, "down_weight": down_weight}


epsilon = 1e-05
root_half = 0.7071067811865476
inv_root_tau = 0.3989422804014327

def gelu_parts(hidden):
    normal_cdf = 0.5 * (1.0 + lax.erf(hidden * root_half))
    density = inv_root_tau * jnp.exp(-0.5 * hidden * hidden)
    return (hidden * normal_cdf, normal_cdf + hidden * density)

def rounded(values):
    return lax.optimization_barrier(values.astype(jnp.bfloat16)).astype(jnp.float32)

def tree_sum(parts_low):
    level_vals = lax.optimization_barrier(parts_low).astype(jnp.float32)
    summed = level_vals[0::2] + level_vals[1::2]
    while summed.shape[0] > 1:
        again = rounded(summed)
        summed = again[0::2] + again[1::2]
    return summed[0]

def reference(tokens, cotangent, routes, ln_gain, ln_bias, router_weight, up_weight, down_weight):
    flight = N_EXPERT // SLICES
    count_tok = tokens.shape[0]
    values = tokens.astype(jnp.float32)
    centre = values - lax.optimization_barrier(jnp.mean(values, axis=1, keepdims=True))
    scale_inv = lax.rsqrt(lax.optimization_barrier(jnp.mean(centre * centre, axis=1, keepdims=True)) + epsilon)
    normed = centre * scale_inv
    gain_f = ln_gain.astype(jnp.float32)
    normal = (normed * gain_f + ln_bias.astype(jnp.float32)).astype(jnp.bfloat16)
    logits = jnp.dot(normal, router_weight, preferred_element_type=jnp.float32)
    first_logit = jnp.take_along_axis(logits, routes[:, 0:1], axis=1)[:, 0]
    second_logit = jnp.take_along_axis(logits, routes[:, 1:2], axis=1)[:, 0]
    score_gap = first_logit - second_logit
    gate_pair = jnp.stack([jax.nn.sigmoid(score_gap), jax.nn.sigmoid(-score_gap)], axis=1)
    flat_ids = routes.reshape(-1)
    row_bound = N_DP * N_EXPERT * CAP
    ff_block = FF // N_DP
    mixed_sum = jnp.zeros((count_tok, D), jnp.float32)
    back_sum = jnp.zeros((count_tok, D), jnp.float32)
    gate_flat = jnp.zeros((count_tok * 2,), jnp.float32)
    up_grads = []
    down_grads = []
    for expert in range(flight):
        row_order = jnp.argsort((flat_ids != expert).astype(jnp.int32), stable=True)[:row_bound].astype(jnp.int32)
        is_valid = flat_ids[row_order] == expert
        valid_f = is_valid.astype(jnp.float32)[:, None]
        tok_index = (row_order // 2).astype(jnp.int32)
        which_slot = (row_order % 2).astype(jnp.int32)
        cot_rows = cotangent[tok_index].astype(jnp.float32)
        rows_in = (normal[tok_index].astype(jnp.float32) * valid_f).astype(jnp.bfloat16)
        rows_grad = (gate_pair[tok_index, which_slot][:, None] * cot_rows * valid_f).astype(jnp.bfloat16)
        up_block = up_weight[expert * SLICES:(expert + 1) * SLICES].astype(jnp.float32)
        down_block = down_weight[expert * SLICES:(expert + 1) * SLICES].astype(jnp.float32)
        in_parts = rows_in.astype(jnp.float32).reshape(row_bound, SLICES, DQ)
        grad_parts = rows_grad.astype(jnp.float32).reshape(row_bound, SLICES, DQ)
        hidden = tree_sum(jnp.einsum('msd,sdf->smf', in_parts, up_block).astype(jnp.bfloat16))
        gelu_value, gelu_slope = gelu_parts(hidden)
        active = gelu_value.astype(jnp.bfloat16)
        active_f = active.astype(jnp.float32)
        down_full = down_block.transpose(1, 0, 2).reshape(FF, D)
        up_full = up_block.reshape(D, FF)
        out_blocks = jnp.einsum('msf,sfd->smd', active_f.reshape(row_bound, N_DP, ff_block), down_full.reshape(N_DP, ff_block, D))
        out_rows = lax.optimization_barrier(jnp.sum(rounded(out_blocks), axis=0)).astype(jnp.bfloat16)
        back_hidden = tree_sum(jnp.einsum('msd,sfd->smf', grad_parts, down_block).astype(jnp.bfloat16))
        grad_hidden = (back_hidden * gelu_slope).astype(jnp.bfloat16)
        grad_hidden_f = grad_hidden.astype(jnp.float32)
        down_grads.append(jnp.einsum('mf,msd->sfd', active_f, grad_parts).astype(jnp.bfloat16))
        up_grads.append(jnp.einsum('msd,mf->sdf', in_parts, grad_hidden_f).astype(jnp.bfloat16))
        back_blocks = jnp.einsum('msf,dsf->smd', grad_hidden_f.reshape(row_bound, N_DP, ff_block), up_full.reshape(D, N_DP, ff_block))
        back_rows = lax.optimization_barrier(jnp.sum(rounded(back_blocks), axis=0)).astype(jnp.bfloat16)
        out_f = out_rows.astype(jnp.float32)
        mixed_sum = mixed_sum.at[tok_index].add(gate_pair[tok_index, which_slot][:, None] * out_f * valid_f)
        gate_flat = gate_flat.at[row_order].add(lax.optimization_barrier(jnp.sum(cot_rows * out_f, axis=1)) * is_valid.astype(jnp.float32))
        back_sum = back_sum.at[tok_index].add(back_rows.astype(jnp.float32) * valid_f)
    moe_out = mixed_sum.astype(jnp.bfloat16)
    grad_gate = gate_flat.reshape(count_tok, 2)
    grad_gap = (grad_gate[:, 0] - grad_gate[:, 1]) * gate_pair[:, 0] * gate_pair[:, 1]
    router_cols = router_weight.T
    first_col = router_cols[routes[:, 0]].astype(jnp.float32)
    second_col = router_cols[routes[:, 1]].astype(jnp.float32)
    grad_normal = back_sum + grad_gap[:, None] * (first_col - second_col)
    expert_ids = jnp.arange(ROUTER, dtype=jnp.int32)
    signed_pick = (routes[:, 0:1] == expert_ids).astype(jnp.float32) - (routes[:, 1:2] == expert_ids).astype(jnp.float32)
    router_term = grad_gap[:, None] * signed_pick
    grad_router = jnp.dot(normal.astype(jnp.float32).T, router_term, precision=lax.Precision.HIGHEST)
    grad_gain = lax.optimization_barrier(jnp.sum(grad_normal * normed, axis=0))
    grad_bias = lax.optimization_barrier(jnp.sum(grad_normal, axis=0))
    grad_norm = grad_normal * gain_f
    grad_input = scale_inv * (grad_norm - lax.optimization_barrier(jnp.mean(grad_norm, axis=1, keepdims=True)) - normed * lax.optimization_barrier(jnp.mean(grad_norm * normed, axis=1, keepdims=True)))
    grad_up = jnp.concatenate(up_grads, axis=0)
    grad_down = jnp.concatenate(down_grads, axis=0)
    return (moe_out, grad_input.astype(jnp.bfloat16), grad_up, grad_down, grad_router, grad_gain, grad_bias)
```

```python
import functools

import jax
import jax.numpy as jnp
from jax import lax
from jax.experimental import pallas as pl
from jax.experimental.pallas import tpu as pltpu
from jax.sharding import PartitionSpec as P

SLICES = 8
CAP = 3
SLOTS = 4
SIDE = 4
GROUP = 16
WIDTH = 256
UNITS = 512
ROWS = 48
CHUNK = SIDE * ROWS
MESH = pl.DeviceIdType.MESH

epsilon = 1e-05
root_half = 0.7071067811865476
inv_root_tau = 0.3989422804014327
f32 = jnp.float32
bf16 = jnp.bfloat16


def gelu_parts(hidden):
    normal_cdf = 0.5 * (1.0 + lax.erf(hidden * root_half))
    density = inv_root_tau * jnp.exp(-0.5 * hidden * hidden)
    return (hidden * normal_cdf, normal_cdf + hidden * density)


class Copies:
    def __init__(self, send_sems, recv_sems):
        self.send_sems, self.recv_sems, self.made = send_sems, recv_sems, []

    def start(self, src, dst, device):
        index = len(self.made)
        copy = pltpu.make_async_remote_copy(
            src_ref=src,
            dst_ref=dst,
            send_sem=self.send_sems.at[index],
            recv_sem=self.recv_sems.at[index],
            device_id=device,
            device_id_type=MESH,
        )
        copy.start()
        self.made.append(copy)
        return copy

    def finish(self):
        for copy in self.made:
            copy.wait_send()


def greet(partners):
    barrier = pltpu.get_barrier_semaphore()
    for device in partners:
        pl.semaphore_signal(barrier, inc=1, device_id=device, device_id_type=MESH)
    pl.semaphore_wait(barrier, len(partners))


def place():
    dp = lax.axis_index("dp")
    ex = lax.axis_index("expert")
    return dp // SIDE, dp % SIDE, ex // 2, ex % 2, dp, ex


def x_partner(step, x, y, ex):
    return (((x + step) % SIDE) * SIDE + y, ex)


def y_partner(step, x, y, ex):
    return (x * SIDE + (y + step) % SIDE, ex)


def gather_kernel(block, out, held, send_sems, recv_sems):
    x, y, z, c, dp, ex = place()
    other = (dp, 2 * z + 1 - c)
    peers = [((dp + step) % GROUP, ex) for step in range(1, GROUP)]
    greet(peers + [other])
    copies = Copies(send_sems, recv_sems)
    sent = [copies.start(block.at[c], held.at[c, dp], peer) for peer in peers]
    held[c, dp] = block[c]
    for copy in sent:
        copy.wait_recv()
    copies.start(held.at[c], held.at[c], other).wait_recv()
    out[...] = held[...]
    copies.finish()


def gather_params(packed):
    return pl.pallas_call(
        gather_kernel,
        out_shape=jax.ShapeDtypeStruct((2, GROUP) + packed.shape[1:], bf16),
        in_specs=[pl.BlockSpec(memory_space=pltpu.VMEM)],
        out_specs=pl.BlockSpec(memory_space=pltpu.VMEM),
        scratch_shapes=[
            pltpu.VMEM((2, GROUP) + packed.shape[1:], bf16),
            pltpu.SemaphoreType.DMA((GROUP,)),
            pltpu.SemaphoreType.DMA((GROUP,)),
        ],
        compiler_params=pltpu.CompilerParams(collective_id=0, has_side_effects=True, vmem_limit_bytes=32 << 20),
    )(packed)


def packing_index(line):
    slot = line & 3
    row = ((line >> 3) & 1) * (2 * ROWS) + ((line >> 2) & 1) * ROWS + (line >> 4) * CAP + slot
    return jnp.where(slot < CAP, row, -1)


def product(left, right, left_dim, right_dim):
    return lax.dot_general(left, right, (((left_dim,), (right_dim,)), ((), ())), preferred_element_type=f32)


def moe_kernel(
    send, w1, w2, wx1, wx2,
    home, gd_own, gd_far, gu_own, gu_far,
    recv, ag, pown, cs, cr, zs, zr, act, gh, slope, part, rs1, mid, rs2, hsend, hrecv,
    send_sems, recv_sems,
):
    x, y, z, c, dp, ex = place()
    half = (z % 4) // 2
    near = z % 2
    me = (z // 4) * 4 + near * 2 + c

    def member(step):
        g = (me + step) % GROUP
        return g, (dp, 2 * (4 * (g // 4) + 2 * half + (g % 4) // 2) + g % 2)

    others = [member(step) for step in range(1, GROUP)]
    along_x = [x_partner(step, x, y, ex) for step in range(1, SIDE)]
    along_y = [y_partner(step, x, y, ex) for step in range(1, SIDE)]
    core = (dp, 2 * z + 1 - c)
    beside = (dp, 2 * (z + 1 - 2 * near) + c)
    greet([device for _, device in others] + along_x + along_y)
    copies = Copies(send_sems, recv_sems)

    sent = [copies.start(send.at[g], recv.at[me], device) for g, device in others]
    recv[me] = send[me]
    lines = lax.broadcasted_iota(jnp.int32, (4 * ROWS, GROUP * 16), 1)
    rows = lax.broadcasted_iota(jnp.int32, (4 * ROWS, GROUP * 16), 0)
    pack = (packing_index(lines) == rows).astype(f32).astype(bf16)
    for copy in sent:
        copy.wait_recv()
    packed = jnp.dot(pack, recv[...].reshape(GROUP * 16, WIDTH), preferred_element_type=f32).astype(bf16)
    for kind in range(2):
        for blk in range(2):
            first = (kind * 2 + blk) * ROWS
            ag[kind, blk, x, y] = packed[first:first + ROWS]

    first_n = [copies.start(ag.at[0, :, x, y], ag.at[0, :, x, y], device) for device in along_y]
    first_s = [copies.start(ag.at[1, :, x, y], ag.at[1, :, x, y], device) for device in along_x]
    low, high = pl.ds(0, 2), pl.ds(2, 2)
    for copy in first_n:
        copy.wait_recv()
    right, left = along_x[0], along_x[2]
    n_1 = copies.start(ag.at[0, :, x, low], ag.at[0, :, x, low], right)
    n_2 = copies.start(ag.at[0, :, x, high], ag.at[0, :, x, high], left)
    n_3 = copies.start(ag.at[0, :, x, high], ag.at[0, :, x, high], right)
    n_4 = copies.start(ag.at[0, :, x, low], ag.at[0, :, x, low], left)
    for copy in first_s:
        copy.wait_recv()
    up, down = along_y[0], along_y[2]
    s_1 = copies.start(ag.at[1, :, low, y], ag.at[1, :, low, y], up)
    s_2 = copies.start(ag.at[1, :, high, y], ag.at[1, :, high, y], down)
    s_3 = copies.start(ag.at[1, :, high, y], ag.at[1, :, high, y], up)
    s_4 = copies.start(ag.at[1, :, low, y], ag.at[1, :, low, y], down)
    x_left, x_right, y_down, y_up = (x + 3) % SIDE, (x + 1) % SIDE, (y + 3) % SIDE, (y + 1) % SIDE
    n_1.wait_recv()
    n_5 = copies.start(ag.at[0, :, x_left, low], ag.at[0, :, x_left, low], right)
    n_2.wait_recv()
    n_6 = copies.start(ag.at[0, :, x_right, high], ag.at[0, :, x_right, high], left)
    s_1.wait_recv()
    s_5 = copies.start(ag.at[1, :, low, y_down], ag.at[1, :, low, y_down], up)
    s_2.wait_recv()
    s_6 = copies.start(ag.at[1, :, high, y_up], ag.at[1, :, high, y_up], down)
    for copy in (n_3, n_4, n_5, n_6):
        copy.wait_recv()

    def rows_of(kind, blk, group):
        return ag[kind, blk, group].reshape(CHUNK, WIDTH)

    def partial_sum(kind, group):
        if kind == 0:
            return product(rows_of(0, 0, group), w1[...], 1, 0) + product(rows_of(0, 1, group), wx1[...], 1, 0)
        return product(rows_of(1, 0, group), w2[...], 1, 1) + product(rows_of(1, 1, group), wx2[...], 1, 1)

    mine = [(x + c) % SIDE, (x + 3 - c) % SIDE]
    theirs = [(x + 1 - c) % SIDE, (x + 2 + c) % SIDE]
    crossed, zoned = {}, {}

    def begin(kind):
        for j in range(2):
            cs[kind, j] = partial_sum(kind, theirs[j]).astype(bf16)
            crossed[kind, j] = copies.start(cs.at[kind, j], cr.at[kind, j], core)
        for j in range(2):
            pown[kind, j] = partial_sum(kind, mine[j])
        for j in range(2):
            crossed[kind, j].wait_recv()
            zs[kind, j] = (pown[kind, j] + cr[kind, j].astype(f32)).astype(bf16)
            zoned[kind, j] = copies.start(zs.at[kind, j], zr.at[kind, j], beside)

    def whole(kind, j):
        zoned[kind, j].wait_recv()
        return zs[kind, j].astype(f32) + zr[kind, j].astype(f32)

    def spread(kind, values_of, weight_a, weight_b, right_dim):
        for group in range(SIDE):
            chunk = values_of[group]
            for blk, weight in ((0, weight_a), (1, weight_b)):
                part[kind, blk, group] = product(chunk, weight[...], 1, right_dim).astype(bf16).reshape(SIDE, ROWS, WIDTH)

    def reduce_first(kind):
        found = []
        for step in range(1, SIDE):
            found.append(copies.start(part.at[kind, 0, (x + step) % SIDE], rs1.at[kind, 0, step - 1], along_x[step - 1]))
            found.append(copies.start(part.at[kind, 1, :, (y + step) % SIDE], rs1.at[kind, 1, step - 1], along_y[step - 1]))
        return found

    def reduce_second(kind, found):
        for copy in found:
            copy.wait_recv()
        for blk in range(2):
            own = part[kind, 0, x] if blk == 0 else part[kind, 1, :, y]
            total = own.astype(f32)
            for step in range(SIDE - 1):
                total = total + rs1[kind, blk, step].astype(f32)
            mid[kind, blk] = total.astype(bf16)
        again = []
        for step in range(1, SIDE):
            again.append(copies.start(mid.at[kind, 0, (y + step) % SIDE], rs2.at[kind, 0, step - 1], along_y[step - 1]))
            again.append(copies.start(mid.at[kind, 1, (x + step) % SIDE], rs2.at[kind, 1, step - 1], along_x[step - 1]))
        return again

    def reduce_last(kind, again):
        for copy in again:
            copy.wait_recv()
        ends = []
        for blk in range(2):
            total = mid[kind, blk, y if blk == 0 else x].astype(f32)
            for step in range(SIDE - 1):
                total = total + rs2[kind, blk, step].astype(f32)
            ends.append(total.astype(bf16))
        return ends

    begin(0)
    for copy in (s_3, s_4, s_5, s_6):
        copy.wait_recv()
    begin(1)
    shared = []
    for j in range(2):
        value, grade = gelu_parts(whole(0, j))
        act[mine[j]] = value.astype(bf16)
        shared.append(copies.start(act.at[mine[j]], act.at[mine[j]], core))
        slope[j] = grade
    for copy in shared:
        copy.wait_recv()
    spread(0, act, w2, wx2, 0)
    found_out = reduce_first(0)
    active = act[...].reshape(SIDE * CHUNK, UNITS)
    gd_own[...] = product(active, ag[1, 0].reshape(SIDE * CHUNK, WIDTH), 0, 0)
    gd_far[...] = product(active, ag[1, 1].reshape(SIDE * CHUNK, WIDTH), 0, 0).astype(bf16)
    shared = []
    for j in range(2):
        gh[mine[j]] = (whole(1, j) * slope[j]).astype(bf16)
        shared.append(copies.start(gh.at[mine[j]], gh.at[mine[j]], core))
    again_out = reduce_second(0, found_out)
    for copy in shared:
        copy.wait_recv()
    spread(1, gh, w1, wx1, 1)
    found_in = reduce_first(1)
    ends = reduce_last(0, again_out)
    grads = gh[...].reshape(SIDE * CHUNK, UNITS)
    gu_own[...] = product(ag[0, 0].reshape(SIDE * CHUNK, WIDTH), grads, 0, 0)
    gu_far[...] = product(ag[0, 1].reshape(SIDE * CHUNK, WIDTH), grads, 0, 0).astype(bf16)
    ends = ends + reduce_last(1, reduce_second(1, found_in))

    lines = lax.broadcasted_iota(jnp.int32, (GROUP * 16, 4 * ROWS), 0)
    rows = lax.broadcasted_iota(jnp.int32, (GROUP * 16, 4 * ROWS), 1)
    unpack = (packing_index(lines) == rows).astype(f32).astype(bf16)
    hsend[...] = (
        jnp.dot(unpack, jnp.concatenate(ends, axis=0), preferred_element_type=f32)
        .astype(bf16)
        .reshape(GROUP, 16, WIDTH)
    )
    sent = [copies.start(hsend.at[g], hrecv.at[me], device) for g, device in others]
    hrecv[me] = hsend[me]
    for copy in sent:
        copy.wait_recv()
    home[...] = hrecv[...]
    copies.finish()


def run_experts(send, w1, w2, wx1, wx2):
    vmem = pl.BlockSpec(memory_space=pltpu.VMEM)
    count = 96
    pair = (2, 2, CHUNK, UNITS)
    return pl.pallas_call(
        moe_kernel,
        out_shape=[
            jax.ShapeDtypeStruct((GROUP, 16, WIDTH), bf16),
            jax.ShapeDtypeStruct((UNITS, WIDTH), f32),
            jax.ShapeDtypeStruct((UNITS, WIDTH), bf16),
            jax.ShapeDtypeStruct((WIDTH, UNITS), f32),
            jax.ShapeDtypeStruct((WIDTH, UNITS), bf16),
        ],
        in_specs=[vmem] * 5,
        out_specs=[vmem] * 5,
        scratch_shapes=[
            pltpu.VMEM((GROUP, 16, WIDTH), bf16),
            pltpu.VMEM((2, 2, SIDE, SIDE, ROWS, WIDTH), bf16),
            pltpu.VMEM(pair, f32),
            pltpu.VMEM(pair, bf16),
            pltpu.VMEM(pair, bf16),
            pltpu.VMEM(pair, bf16),
            pltpu.VMEM(pair, bf16),
            pltpu.VMEM((SIDE, CHUNK, UNITS), bf16),
            pltpu.VMEM((SIDE, CHUNK, UNITS), bf16),
            pltpu.VMEM((2, CHUNK, UNITS), f32),
            pltpu.VMEM((2, 2, SIDE, SIDE, ROWS, WIDTH), bf16),
            pltpu.VMEM((2, 2, SIDE - 1, SIDE, ROWS, WIDTH), bf16),
            pltpu.VMEM((2, 2, SIDE, ROWS, WIDTH), bf16),
            pltpu.VMEM((2, 2, SIDE - 1, ROWS, WIDTH), bf16),
            pltpu.VMEM((GROUP, 16, WIDTH), bf16),
            pltpu.VMEM((GROUP, 16, WIDTH), bf16),
            pltpu.SemaphoreType.DMA((count,)),
            pltpu.SemaphoreType.DMA((count,)),
        ],
        compiler_params=pltpu.CompilerParams(collective_id=1, has_side_effects=True, vmem_limit_bytes=48 << 20),
    )(send, w1, w2, wx1, wx2)


def reduce_kernel(parts, out, cr, s0, r1, s1, r2, s2, r3, s3, r4, fin, send_sems, recv_sems):
    x, y, z, c, dp, ex = place()
    outer, inner = z // SIDE, z % SIDE
    core = (dp, 2 * z + 1 - c)
    along_x = [x_partner(step, x, y, ex) for step in range(1, SIDE)]
    along_y = [y_partner(step, x, y, ex) for step in range(1, SIDE)]
    along_in = [(dp, 2 * (outer * SIDE + (inner + step) % SIDE) + c) for step in range(1, SIDE)]
    along_out = [(dp, 2 * ((outer + step) % SIDE * SIDE + inner) + c) for step in range(1, SIDE)]
    greet([core] + along_x + along_y + along_in + along_out)
    copies = Copies(send_sems, recv_sems)
    copies.start(parts.at[1 - c], cr, core).wait_recv()
    s0[...] = (parts[c].astype(f32) + cr[...].astype(f32)).astype(bf16)
    sent = []
    for step in range(1, SIDE):
        sent.append(copies.start(s0.at[0, (x + step) % SIDE], r1.at[0, step - 1], along_x[step - 1]))
        sent.append(copies.start(s0.at[1, :, (y + step) % SIDE], r1.at[1, step - 1], along_y[step - 1]))
    for copy in sent:
        copy.wait_recv()
    for path in range(2):
        own = s0[0, x] if path == 0 else s0[1, :, y]
        s1[path] = (own.astype(f32) + r1[path, 0].astype(f32) + r1[path, 1].astype(f32) + r1[path, 2].astype(f32)).astype(bf16)
    sent = []
    for step in range(1, SIDE):
        sent.append(copies.start(s1.at[0, (y + step) % SIDE], r2.at[0, step - 1], along_y[step - 1]))
        sent.append(copies.start(s1.at[1, (x + step) % SIDE], r2.at[1, step - 1], along_x[step - 1]))
    for copy in sent:
        copy.wait_recv()
    for path in range(2):
        own = s1[path, y if path == 0 else x]
        s2[path] = (own.astype(f32) + r2[path, 0].astype(f32) + r2[path, 1].astype(f32) + r2[path, 2].astype(f32)).astype(bf16)
    sent = [copies.start(s2, r3.at[inner], device) for device in along_in]
    r3[inner] = s2[...]
    for copy in sent:
        copy.wait_recv()
    s3[...] = (
        (r3[0].astype(f32) + r3[1].astype(f32)) + (r3[2].astype(f32) + r3[3].astype(f32))
    ).astype(bf16)
    sent = [copies.start(s3, r4.at[outer], device) for device in along_out]
    r4[outer] = s3[...]
    for copy in sent:
        copy.wait_recv()
    fin[c] = ((r4[0].astype(f32) + r4[1].astype(f32)) + (r4[2].astype(f32) + r4[3].astype(f32))).astype(bf16)
    copies.start(fin.at[c], fin.at[c], core).wait_recv()
    out[...] = fin[...].astype(f32)
    copies.finish()


def reduce_dense(parts):
    tall = parts.shape[-2]
    block = (tall, 128)
    return pl.pallas_call(
        reduce_kernel,
        out_shape=jax.ShapeDtypeStruct((2, 2) + block, f32),
        in_specs=[pl.BlockSpec(memory_space=pltpu.VMEM)],
        out_specs=pl.BlockSpec(memory_space=pltpu.VMEM),
        scratch_shapes=[
            pltpu.VMEM((2, SIDE, SIDE) + block, bf16),
            pltpu.VMEM((2, SIDE, SIDE) + block, bf16),
            pltpu.VMEM((2, SIDE - 1, SIDE) + block, bf16),
            pltpu.VMEM((2, SIDE) + block, bf16),
            pltpu.VMEM((2, SIDE - 1) + block, bf16),
            pltpu.VMEM((2,) + block, bf16),
            pltpu.VMEM((SIDE, 2) + block, bf16),
            pltpu.VMEM((2,) + block, bf16),
            pltpu.VMEM((SIDE, 2) + block, bf16),
            pltpu.VMEM((2, 2) + block, bf16),
            pltpu.SemaphoreType.DMA((24,)),
            pltpu.SemaphoreType.DMA((24,)),
        ],
        compiler_params=pltpu.CompilerParams(collective_id=2, has_side_effects=True, vmem_limit_bytes=32 << 20),
    )(parts)


def on_device(tokens, cotangent, routes, ln_gain, ln_bias, router_weight, up_weight, down_weight):
    count_tok, feature_count = tokens.shape
    columns = lax.axis_size("expert")
    flight = columns // SLICES
    place_z = lax.axis_index("expert") // 2
    half = (place_z % 4) // 2

    swap = [(i, ((i // 2) ^ 2) * 2 + i % 2) for i in range(columns)]
    w_in, w_out = up_weight[0], down_weight[0]
    far_in = lax.ppermute(w_in, "expert", swap)
    far_out = lax.ppermute(w_out, "expert", swap)

    packed = jnp.concatenate(
        [router_weight, ln_gain[None], ln_bias[None], jnp.zeros((30, 128), bf16)], axis=0
    ).reshape(2, 80, 128)
    params = gather_params(packed)
    params = params.transpose(1, 0, 2, 3).reshape(GROUP, 160, 128)
    router_all = params[:, :128].reshape(feature_count, 128)
    gain_f = params[:, 128].reshape(feature_count).astype(f32)
    bias_f = params[:, 129].reshape(feature_count).astype(f32)

    values = tokens.astype(f32)
    centre = values - jnp.mean(values, axis=1, keepdims=True)
    scale_inv = lax.rsqrt(jnp.mean(centre * centre, axis=1, keepdims=True) + epsilon)
    normed = centre * scale_inv
    normal = (normed * gain_f + bias_f).astype(bf16)
    logits = jnp.dot(normal, router_all, preferred_element_type=f32)
    expert_ids = jnp.arange(router_all.shape[1], dtype=jnp.int32)
    signed_pick = (routes[:, 0:1] == expert_ids).astype(f32) - (routes[:, 1:2] == expert_ids).astype(f32)
    score_gap = jnp.sum(logits * signed_pick, axis=1)
    gate_first, gate_second = jax.nn.sigmoid(score_gap), jax.nn.sigmoid(-score_gap)

    in_flight = jnp.arange(flight, dtype=jnp.int32)
    hits = [(routes[:, k:k + 1] == in_flight).astype(f32) for k in range(2)]
    either = hits[0] + hits[1]
    before = jnp.arange(count_tok)[:, None] > jnp.arange(count_tok)[None, :]
    earlier = jnp.dot(before.astype(bf16), either.astype(bf16), preferred_element_type=f32)
    slot_ids = jnp.arange(SLOTS, dtype=jnp.int32).astype(f32)
    placing = []
    for k in range(2):
        placed = hits[k].T[:, None, :] * (earlier.T[:, None, :] == slot_ids[None, :, None]).astype(f32)
        placing.append(placed.reshape(flight * SLOTS, count_tok))
    place_all = (placing[0] + placing[1]).astype(bf16)
    sel_normal = jnp.dot(place_all, normal, preferred_element_type=f32)
    sel_cot = jnp.dot(place_all, cotangent, preferred_element_type=f32)
    gate_row = jnp.sum(placing[0] * gate_first[None] + placing[1] * gate_second[None], axis=1, keepdims=True)
    both = jnp.stack([sel_normal, gate_row * sel_cot], axis=0).astype(bf16)
    both = both.reshape(2, flight, SLOTS, 2, 4, WIDTH)
    both = jnp.where(half == 1, both[:, :, :, ::-1], both)
    send = both.transpose(1, 4, 0, 3, 2, 5).reshape(GROUP, 16, WIDTH)

    home, gd_own, gd_far, gu_own, gu_far = run_experts(send, w_in, w_out, far_in, far_out)
    gd_back = lax.ppermute(gd_far, "expert", swap)
    gu_back = lax.ppermute(gu_far, "expert", swap)
    grad_down = (gd_own + gd_back.astype(f32)).astype(bf16)[None]
    grad_up = (gu_own + gu_back.astype(f32)).astype(bf16)[None]

    home = home.reshape(flight, 4, 2, 2, SLOTS, WIDTH)
    home = jnp.where(half == 1, home[:, :, :, ::-1], home)
    home = home.transpose(2, 0, 4, 3, 1, 5).reshape(2, flight * SLOTS, feature_count)
    back_out, back_in = home[0], home[1]

    def pick(matrix, rows):
        return lax.dot_general(matrix.astype(bf16), rows, (((0,), (0,)), ((), ())), preferred_element_type=f32)

    moe_out = (
        gate_first[:, None] * pick(placing[0], back_out) + gate_second[:, None] * pick(placing[1], back_out)
    ).astype(bf16)
    row_dot = jnp.sum(sel_cot * back_out.astype(f32), axis=1, keepdims=True)
    gap_raw = jnp.sum((placing[0] - placing[1]) * row_dot, axis=0)
    grad_gap = gap_raw * gate_first * gate_second
    router_pull = lax.dot_general(
        signed_pick.astype(bf16), router_all, (((1,), (1,)), ((), ())), preferred_element_type=f32
    )
    grad_normal = pick(placing[0] + placing[1], back_in) + grad_gap[:, None] * router_pull
    router_term = (grad_gap[:, None] * signed_pick).astype(bf16)
    local_router = lax.dot_general(
        normal, router_term, (((0,), (0,)), ((), ())), preferred_element_type=f32
    ).astype(bf16)
    local_gain = jnp.sum(grad_normal * normed, axis=0).astype(bf16)
    local_bias = jnp.sum(grad_normal, axis=0).astype(bf16)
    parts = jnp.concatenate(
        [
            local_router.reshape(GROUP, 128, 128),
            local_gain.reshape(GROUP, 1, 128),
            local_bias.reshape(GROUP, 1, 128),
            jnp.zeros((GROUP, 62, 128), bf16),
        ],
        axis=1,
    )
    parts = parts.reshape(SIDE, SIDE, 2, 2, 48, 128).transpose(2, 3, 0, 1, 4, 5)
    dense = reduce_dense(parts).reshape(192, 128)

    grad_norm = grad_normal * gain_f
    grad_input = scale_inv * (
        grad_norm
        - jnp.mean(grad_norm, axis=1, keepdims=True)
        - normed * jnp.mean(grad_norm * normed, axis=1, keepdims=True)
    )
    return (moe_out, grad_input.astype(bf16), grad_up, grad_down, dense[:128], dense[128], dense[129])


def solution(mesh):
    return jax.shard_map(
        on_device,
        mesh=mesh,
        in_specs=(
            P(("dp", "expert"), None),
            P(("dp", "expert"), None),
            P(("dp", "expert"), None),
            P("dp"),
            P("dp"),
            P("dp", None),
            P("expert", None, "dp"),
            P("expert", "dp", None),
        ),
        out_specs=(
            P(("dp", "expert"), None),
            P(("dp", "expert"), None),
            P("expert", None, "dp"),
            P("expert", "dp", None),
            P("dp", None),
            P("dp"),
            P("dp"),
        ),
        check_vma=False,
    )
```

```python
import jax
import jax.numpy as jnp
from jax import lax
from jax.experimental import pallas as pl
from jax.experimental.pallas import tpu as pltpu
from jax.sharding import PartitionSpec as P

SLICES = 8
CAP = 3
SLOTS = 4
SIDE = 4
GROUP = 16
WIDTH = 256
LANES = 128
HIDDEN = 2048
TOKENS = 128
UNITS = 512
ROWS = 48
CHUNK = SIDE * ROWS
MESH = pl.DeviceIdType.MESH

epsilon = 1e-05
root_half = 0.7071067811865476
inv_root_tau = 0.3989422804014327
f32 = jnp.float32
bf16 = jnp.bfloat16


def gelu_parts(hidden):
    normal_cdf = 0.5 * (1.0 + lax.erf(hidden * root_half))
    density = inv_root_tau * jnp.exp(-0.5 * hidden * hidden)
    return (hidden * normal_cdf, normal_cdf + hidden * density)


class Copies:
    def __init__(self, send_sems, recv_sems):
        self.send_sems, self.recv_sems, self.made = send_sems, recv_sems, []

    def start(self, src, dst, device):
        index = len(self.made)
        copy = pltpu.make_async_remote_copy(
            src_ref=src,
            dst_ref=dst,
            send_sem=self.send_sems.at[index],
            recv_sem=self.recv_sems.at[index],
            device_id=device,
            device_id_type=MESH,
        )
        copy.start()
        self.made.append(copy)
        return copy

    def finish(self):
        for copy in self.made:
            copy.wait_send()


def place():
    dp = lax.axis_index("dp")
    ex = lax.axis_index("expert")
    return dp // SIDE, dp % SIDE, ex // 2, ex % 2, dp, ex


def x_partner(step, x, y, ex):
    return (((x + step) % SIDE) * SIDE + y, ex)


def y_partner(step, x, y, ex):
    return (x * SIDE + (y + step) % SIDE, ex)


def product(left, right, left_dim, right_dim):
    return lax.dot_general(left, right, (((left_dim,), (right_dim,)), ((), ())), preferred_element_type=f32)


def iota(shape, dim):
    return lax.broadcasted_iota(jnp.int32, shape, dim)


def one_hot(found):
    return found.astype(f32).astype(bf16)


def message_row(row):
    slot, expert = row & 3, (row >> 2) & 3
    lane_half, k2, blk = (row >> 4) & 1, (row >> 5) & 3, row >> 7
    return (expert * 4 + k2) * 16 + blk * 8 + lane_half * 4 + slot


def packed_row(row, lane_half):
    slot = row & 3
    good = (slot < CAP) & (((row >> 2) & 1) == lane_half)
    return jnp.where(good, ((row >> 3) & 1) * ROWS + (row >> 4) * CAP + slot, -1)


def step_kernel(
    tokens, cot, routes, gain, bias, router, w1, w2,
    moe_out, grad_in, gu_out, gd_out, router_out, dense_out,
    normed, block, held, rt, sends, recvs, ag, wx1, wx2, pown, cs, cr, zs, zr, act, gh, slope, part, rs1, mid, rs2,
    hsend, hrecv, gds, gdr, gus, gur, gd_own, gu_own, base,
    lr, lc, l0, l1, l2, l3, l4, l5, l6, l7, l8, fin, gb, gbr, gb1, gb2, gb3,
    send_sems, recv_sems,
):
    x, y, z, c, dp, ex = place()
    outer, inner = z // 4, z % 4
    half, near = inner // 2, inner % 2
    me = outer * 4 + near * 2 + c

    def member(step):
        g = (me + step) % GROUP
        return g, (dp, 2 * (4 * (g // 4) + 2 * half + (g % 4) // 2) + g % 2)

    others = [member(step) for step in range(1, GROUP)]
    peers = [((dp + step) % GROUP, ex) for step in range(1, GROUP)]
    along_x = [x_partner(step, x, y, ex) for step in range(1, SIDE)]
    along_y = [y_partner(step, x, y, ex) for step in range(1, SIDE)]
    core = (dp, 2 * z + 1 - c)
    beside = (dp, 2 * (z + 1 - 2 * near) + c)
    over = (dp, 2 * (z + 2 - 4 * half) + c)
    along_in = [(dp, 2 * (outer * 4 + (inner + step) % 4) + c) for step in range(1, 4)]
    along_out = [(dp, 2 * ((outer + step) % 4 * 4 + inner) + c) for step in range(1, 4)]
    octet = [(dp, 8 * outer + (2 * inner + c + step) % 8) for step in range(1, 8)]
    far_half = [(dp, 2 * (4 * outer + 2 * (1 - half) + k) + d) for k in range(2) for d in range(2)]

    barrier = pltpu.get_barrier_semaphore()
    greeted = [device for _, device in others] + [device for device in peers] + far_half
    for device in greeted:
        pl.semaphore_signal(barrier, inc=1, device_id=device, device_id_type=MESH)

    values = tokens[...].astype(f32)
    centre = values - jnp.mean(values, axis=1, keepdims=True)
    scale_inv = lax.rsqrt(jnp.mean(centre * centre, axis=1, keepdims=True) + epsilon)
    normed[...] = centre * scale_inv
    square = (TOKENS, TOKENS)
    lane, line = iota(square, 1), iota(square, 0)
    first, second = routes[:, 0:1], routes[:, 1:2]
    signed = (first == lane).astype(f32) - (second == lane).astype(f32)
    hit_first = (first == (lane >> 2)).astype(f32) * (lane < 16).astype(f32)
    hit_second = (second == (lane >> 2)).astype(f32) * (lane < 16).astype(f32)
    earlier = product(one_hot(line > lane), (hit_first + hit_second).astype(bf16), 1, 0)
    fits = (earlier == (lane & 3).astype(f32)).astype(f32)
    place_first, place_second = (hit_first * fits).astype(bf16), (hit_second * fits).astype(bf16)
    place_all = place_first + place_second
    arrange = (256, 256)
    to_message = one_hot(message_row(iota(arrange, 1)) == iota(arrange, 0))
    from_message = one_hot(message_row(iota(arrange, 0)) == iota(arrange, 1))
    pack = [one_hot(packed_row(iota((2 * ROWS, 256), 1), part_) == iota((2 * ROWS, 256), 0)) for part_ in range(2)]
    unpack = [one_hot(packed_row(iota((256, 2 * ROWS), 0), part_) == iota((256, 2 * ROWS), 1)) for part_ in range(2)]

    def messages(kind, chosen):
        low, high = chosen[:16, :HIDDEN // 2], chosen[:16, HIDDEN // 2:]
        sides = (jnp.where(half == 1, high, low), jnp.where(half == 1, low, high))
        stacked = jnp.concatenate(
            [side[:, LANES * i:LANES * (i + 1)] for side in sides for i in range(8)], axis=0
        ).astype(bf16)
        sends[kind] = product(to_message, stacked, 1, 0).astype(bf16).reshape(GROUP, 16, LANES)

    def returned(kind):
        stacked = product(from_message, hrecv[kind].reshape(256, LANES), 1, 0).astype(bf16).astype(f32)
        sides = [
            jnp.concatenate([stacked[16 * (8 * blk + i):16 * (8 * blk + i + 1)] for i in range(8)], axis=1)
            for blk in range(2)
        ]
        low, high = jnp.where(half == 1, sides[1], sides[0]), jnp.where(half == 1, sides[0], sides[1])
        rows = jnp.concatenate([low, high], axis=1)
        return jnp.concatenate([rows, jnp.zeros((TOKENS - 16, HIDDEN), f32)], axis=0).astype(bf16)

    messages(0, product(place_all, normed[...].astype(bf16), 0, 0))
    both = (16, LANES)
    edge = jnp.where(iota(both, 0) == 0, gain[...].astype(f32), jnp.where(iota(both, 0) == 1, bias[...].astype(f32), 0.0))
    for side in range(2):
        block[side, 0:64] = router[64 * side:64 * (side + 1)]
        block[side, 64:80] = edge.astype(bf16)
    held[c, dp] = block[c]
    recvs[0, me] = sends[0, me]

    pl.semaphore_wait(barrier, len(greeted))
    copies = Copies(send_sems, recv_sems)
    sent_n = [copies.start(sends.at[0, g], recvs.at[0, me], device) for g, device in others]
    sent_p = [copies.start(block.at[c], held.at[c, dp], peer) for peer in peers]
    got_w1 = copies.start(w1, wx1, over)
    got_w2 = copies.start(w2, wx2, over)

    def wait_for(found):
        for copy in found:
            copy.wait_recv()

    def place_rows(kind, feature_rows):
        for blk in range(2):
            ag[kind, blk, x, y] = feature_rows[blk].astype(bf16)

    def packed_rows(kind):
        rows = recvs[kind].reshape(256, LANES)
        both_halves = jnp.concatenate([product(pack[0], rows, 1, 0), product(pack[1], rows, 1, 0)], axis=1)
        return [both_halves[:ROWS], both_halves[ROWS:]]

    def gather_first(kind):
        return [copies.start(ag.at[kind, 0, x, y], ag.at[kind, 0, x, y], device) for device in along_y] + [
            copies.start(ag.at[kind, 1, x, y], ag.at[kind, 1, x, y], device) for device in along_x
        ]

    x_left, x_right, y_down, y_up = (x + 3) % SIDE, (x + 1) % SIDE, (y + 3) % SIDE, (y + 1) % SIDE
    pairs = (pl.ds(0, 2), pl.ds(2, 2))

    def gather_second(kind):
        def at(blk, place_, which):
            return ag.at[kind, 0, place_, pairs[which]] if blk == 0 else ag.at[kind, 1, pairs[which], place_]

        own, before, after = (x, y), (x_left, y_down), (x_right, y_up)
        ahead, back = (along_x[0], along_y[0]), (along_x[2], along_y[2])

        def move(blk, place_, which, device):
            return copies.start(at(blk, place_, which), at(blk, place_, which), device)

        one = [move(blk, own[blk], 0, ahead[blk]) for blk in range(2)]
        two = [move(blk, own[blk], 1, back[blk]) for blk in range(2)]
        rest = [move(blk, own[blk], 1, ahead[blk]) for blk in range(2)]
        rest += [move(blk, own[blk], 0, back[blk]) for blk in range(2)]
        for blk in range(2):
            one[blk].wait_recv()
            rest.append(move(blk, before[blk], 0, ahead[blk]))
        for blk in range(2):
            two[blk].wait_recv()
            rest.append(move(blk, after[blk], 1, back[blk]))
        return rest

    wait_for(sent_p)
    swap_router = copies.start(held.at[c], held.at[c], core)
    wait_for(sent_n)
    scaled_rows = []
    for blk, rows in enumerate(packed_rows(0)):
        spot = 2 * (4 * (half if blk == 0 else 1 - half) + near * 2 + c)
        parts = [held[c, spot + i, 64:80].astype(f32) for i in range(2)]
        gains = jnp.concatenate([parts[0][0:1], parts[1][0:1]], axis=1)
        biases = jnp.concatenate([parts[0][1:2], parts[1][1:2]], axis=1)
        scaled_rows.append(rows * gains + biases)
    place_rows(0, scaled_rows)
    begun_n = gather_first(0)

    swap_router.wait_recv()
    for block_id in range(GROUP):
        for side in range(2):
            rt[128 * block_id + 64 * side:128 * block_id + 64 * (side + 1)] = held[side, block_id, 0:64]
    gain_all = jnp.concatenate([held[0, i, 64:80].astype(f32)[0:1] for i in range(GROUP)], axis=1)
    bias_all = jnp.concatenate([held[0, i, 64:80].astype(f32)[1:2] for i in range(GROUP)], axis=1)
    normal = (normed[...] * gain_all + bias_all).astype(bf16)
    logits = product(normal, rt[...], 1, 0)
    gap = jnp.sum(logits * signed, axis=1, keepdims=True)
    gate_first, gate_second = jax.nn.sigmoid(gap), jax.nn.sigmoid(-gap)
    cot_f = cot[...].astype(f32)
    messages(
        1,
        product(place_first, (gate_first * cot_f).astype(bf16), 0, 0)
        + product(place_second, (gate_second * cot_f).astype(bf16), 0, 0),
    )
    recvs[1, me] = sends[1, me]
    sent_s = [copies.start(sends.at[1, g], recvs.at[1, me], device) for g, device in others]
    wait_for(begun_n)
    rest_n = gather_second(0)
    wait_for(rest_n)

    def rows_of(kind, blk, group):
        return ag[kind, blk, group].reshape(CHUNK, WIDTH)

    def partial_sum(kind, group):
        if kind == 0:
            return product(rows_of(0, 0, group), w1[...], 1, 0) + product(rows_of(0, 1, group), wx1[...], 1, 0)
        return product(rows_of(1, 0, group), w2[...], 1, 1) + product(rows_of(1, 1, group), wx2[...], 1, 1)

    mine = [(x + c) % SIDE, (x + 3 - c) % SIDE]
    theirs = [(x + 1 - c) % SIDE, (x + 2 + c) % SIDE]
    zoned = {}

    def begin(kind):
        crossed = []
        for j in range(2):
            cs[kind, j] = partial_sum(kind, theirs[j]).astype(bf16)
            crossed.append(copies.start(cs.at[kind, j], cr.at[kind, j], core))
        for j in range(2):
            pown[kind, j] = partial_sum(kind, mine[j])
        for j in range(2):
            crossed[j].wait_recv()
            zs[kind, j] = (pown[kind, j] + cr[kind, j].astype(f32)).astype(bf16)
            zoned[kind, j] = copies.start(zs.at[kind, j], zr.at[kind, j], beside)

    def whole(kind, j):
        zoned[kind, j].wait_recv()
        return zs[kind, j].astype(f32) + zr[kind, j].astype(f32)

    def spread(kind, values_of, weight_a, weight_b, right_dim):
        for group in range(SIDE):
            chunk = values_of[group]
            for blk, weight in ((0, weight_a), (1, weight_b)):
                part[kind, blk, group] = product(chunk, weight[...], 1, right_dim).astype(bf16).reshape(SIDE, ROWS, WIDTH)

    def reduce_first(kind):
        found = []
        for step in range(1, SIDE):
            found.append(copies.start(part.at[kind, 0, (x + step) % SIDE], rs1.at[kind, 0, step - 1], along_x[step - 1]))
            found.append(copies.start(part.at[kind, 1, :, (y + step) % SIDE], rs1.at[kind, 1, step - 1], along_y[step - 1]))
        return found

    def reduce_second(kind, found):
        wait_for(found)
        for blk in range(2):
            own = part[kind, 0, x] if blk == 0 else part[kind, 1, :, y]
            total = own.astype(f32)
            for step in range(SIDE - 1):
                total = total + rs1[kind, blk, step].astype(f32)
            mid[kind, blk] = total.astype(bf16)
        again = []
        for step in range(1, SIDE):
            again.append(copies.start(mid.at[kind, 0, (y + step) % SIDE], rs2.at[kind, 0, step - 1], along_y[step - 1]))
            again.append(copies.start(mid.at[kind, 1, (x + step) % SIDE], rs2.at[kind, 1, step - 1], along_x[step - 1]))
        return again

    def send_home(kind, again):
        wait_for(again)
        ends = []
        for blk in range(2):
            total = mid[kind, blk, y if blk == 0 else x].astype(f32)
            for step in range(SIDE - 1):
                total = total + rs2[kind, blk, step].astype(f32)
            ends.append(total.astype(bf16))
        rows = jnp.concatenate(ends, axis=0)
        out = product(unpack[0], rows[:, :LANES], 1, 0) + product(unpack[1], rows[:, LANES:], 1, 0)
        hsend[kind] = out.astype(bf16).reshape(GROUP, 16, LANES)
        hrecv[kind, me] = hsend[kind, me]
        return [copies.start(hsend.at[kind, g], hrecv.at[kind, me], device) for g, device in others]

    got_w1.wait_recv()
    begin(0)
    wait_for(sent_s)
    place_rows(1, packed_rows(1))
    wait_for(gather_first(1))
    wait_for(gather_second(1))
    got_w2.wait_recv()
    begin(1)
    shared = []
    for j in range(2):
        value, grade = gelu_parts(whole(0, j))
        act[mine[j]] = value.astype(bf16)
        shared.append(copies.start(act.at[mine[j]], act.at[mine[j]], core))
        slope[j] = grade
    wait_for(shared)
    spread(0, act, w2, wx2, 0)
    found_out = reduce_first(0)
    active = act[...].reshape(SIDE * CHUNK, UNITS)
    gds[...] = product(active, ag[1, 1].reshape(SIDE * CHUNK, WIDTH), 0, 0).astype(bf16)
    got_gd = copies.start(gds, gdr, over)
    gd_own[...] = product(active, ag[1, 0].reshape(SIDE * CHUNK, WIDTH), 0, 0)
    again_out = reduce_second(0, found_out)
    shared = []
    for j in range(2):
        gh[mine[j]] = (whole(1, j) * slope[j]).astype(bf16)
        shared.append(copies.start(gh.at[mine[j]], gh.at[mine[j]], core))
    home_out = send_home(0, again_out)
    wait_for(shared)
    spread(1, gh, w1, wx1, 1)
    found_in = reduce_first(1)
    grads = gh[...].reshape(SIDE * CHUNK, UNITS)
    gus[...] = product(ag[0, 1].reshape(SIDE * CHUNK, WIDTH), grads, 0, 0).astype(bf16)
    got_gu = copies.start(gus, gur, over)
    gu_own[...] = product(ag[0, 0].reshape(SIDE * CHUNK, WIDTH), grads, 0, 0)

    wait_for(home_out)
    rows = returned(0)
    out_first, out_second = product(place_first, rows, 1, 0), product(place_second, rows, 1, 0)
    moe_out[...] = (gate_first * out_first + gate_second * out_second).astype(bf16)
    gap_grad = jnp.sum(cot[...].astype(f32) * (out_first - out_second), axis=1, keepdims=True) * gate_first * gate_second
    base[...] = gap_grad * product(signed.astype(bf16), rt[...], 1, 1)
    normal = (normed[...] * gain_all + bias_all).astype(bf16)
    local = product(normal, (gap_grad * signed).astype(bf16), 0, 0).astype(bf16)
    for block_id in range(GROUP):
        for side in range(2):
            for path in range(2):
                begin_row = 128 * block_id + 64 * side + 32 * path
                lr[side, path, block_id // SIDE, block_id % SIDE] = local[begin_row:begin_row + 32]

    cored = copies.start(lr.at[1 - c], lc, core)
    again_in = reduce_second(1, found_in)
    cored.wait_recv()
    l0[...] = (lr[c].astype(f32) + lc[...].astype(f32)).astype(bf16)
    sent = []
    for step in range(1, SIDE):
        sent.append(copies.start(l0.at[0, (x + step) % SIDE], l1.at[0, step - 1], along_x[step - 1]))
        sent.append(copies.start(l0.at[1, :, (y + step) % SIDE], l1.at[1, step - 1], along_y[step - 1]))
    home_in = send_home(1, again_in)
    wait_for(sent)
    for path in range(2):
        own = l0[0, x] if path == 0 else l0[1, :, y]
        l2[path] = (own.astype(f32) + l1[path, 0].astype(f32) + l1[path, 1].astype(f32) + l1[path, 2].astype(f32)).astype(bf16)
    sent = []
    for step in range(1, SIDE):
        sent.append(copies.start(l2.at[0, (y + step) % SIDE], l3.at[0, step - 1], along_y[step - 1]))
        sent.append(copies.start(l2.at[1, (x + step) % SIDE], l3.at[1, step - 1], along_x[step - 1]))
    wait_for(sent)
    for path in range(2):
        own = l2[path, y if path == 0 else x]
        total = (own.astype(f32) + l3[path, 0].astype(f32)) + (l3[path, 1].astype(f32) + l3[path, 2].astype(f32))
        l4[2 * path] = total[0:16].astype(bf16)
        l4[2 * path + 1] = total[16:32].astype(bf16)
    sent_l = [copies.start(l4.at[(inner + step) % 4], l5.at[step - 1], along_in[step - 1]) for step in range(1, 4)]

    wait_for(home_in)
    grad_normal = product(place_all, returned(1), 1, 0) + base[...]
    gains = jnp.sum(grad_normal * normed[...], axis=0, keepdims=True)
    biases = jnp.sum(grad_normal, axis=0, keepdims=True)
    wide = (8, HIDDEN)
    dense = jnp.where(iota(wide, 0) == 0, gains, jnp.where(iota(wide, 0) == 1, biases, 0.0))
    for block_id in range(GROUP):
        gb[block_id] = dense[:, 128 * block_id:128 * (block_id + 1)]
    sent_g = [
        copies.start(gb.at[(dp + step) % GROUP], gbr.at[step - 1], peer) for step, peer in enumerate(peers, 1)
    ]
    wait_for(sent_l)
    l6[...] = (
        (l4[inner].astype(f32) + l5[0].astype(f32)) + (l5[1].astype(f32) + l5[2].astype(f32))
    ).astype(bf16)
    sent_l = [copies.start(l6, l7.at[outer], device) for device in along_out]
    l7[outer] = l6[...]
    grad_norm = grad_normal * gain_all
    mean_grad = jnp.mean(grad_norm, axis=1, keepdims=True)
    mean_both = jnp.mean(grad_norm * normed[...], axis=1, keepdims=True)
    grad_in[...] = (scale_inv * (grad_norm - mean_grad - normed[...] * mean_both)).astype(bf16)
    wait_for(sent_g)
    total = gb[dp]
    for step in range(GROUP - 1):
        total = total + gbr[step]
    gb1[...] = total
    gb2[2 * inner + c] = total
    sent_g = [copies.start(gb1, gb2.at[2 * inner + c], device) for device in octet]
    wait_for(sent_l)
    l8[inner] = ((l7[0].astype(f32) + l7[1].astype(f32)) + (l7[2].astype(f32) + l7[3].astype(f32))).astype(bf16)
    sent_l = [copies.start(l8.at[inner], l8.at[inner], device) for device in along_in]
    wait_for(sent_g)
    total = gb2[0]
    for i in range(1, 8):
        total = total + gb2[i]
    gb3[outer] = total
    sent_g = [copies.start(gb3.at[outer], gb3.at[outer], device) for device in along_out]
    got_gd.wait_recv()
    gd_out[...] = (gd_own[...] + gdr[...].astype(f32)).astype(bf16)
    wait_for(sent_l)
    fin[c] = l8[...]
    last = copies.start(fin.at[c], fin.at[c], core)
    got_gu.wait_recv()
    gu_out[...] = (gu_own[...] + gur[...].astype(f32)).astype(bf16)
    wait_for(sent_g)
    dense_out[...] = (gb3[0] + gb3[1]) + (gb3[2] + gb3[3])
    last.wait_recv()
    router_out[...] = fin[...].astype(f32).reshape(128, 128)
    copies.finish()


def on_device(tokens, cotangent, routes, ln_gain, ln_bias, router_weight, up_weight, down_weight):
    vmem = pl.BlockSpec(memory_space=pltpu.VMEM)
    pair = (2, 2, CHUNK, UNITS)
    moved = (2, 2, SIDE, SIDE, ROWS, WIDTH)
    dense = (8, LANES)
    scratch = [
        ((TOKENS, HIDDEN), f32),
        ((2, 80, LANES), bf16),
        ((2, GROUP, 80, LANES), bf16),
        ((HIDDEN, LANES), bf16),
        ((2, GROUP, 16, LANES), bf16),
        ((2, GROUP, 16, LANES), bf16),
        (moved, bf16),
        ((WIDTH, UNITS), bf16),
        ((UNITS, WIDTH), bf16),
        (pair, f32),
        (pair, bf16),
        (pair, bf16),
        (pair, bf16),
        (pair, bf16),
        ((SIDE, CHUNK, UNITS), bf16),
        ((SIDE, CHUNK, UNITS), bf16),
        ((2, CHUNK, UNITS), f32),
        (moved, bf16),
        ((2, 2, SIDE - 1, SIDE, ROWS, WIDTH), bf16),
        ((2, 2, SIDE, ROWS, WIDTH), bf16),
        ((2, 2, SIDE - 1, ROWS, WIDTH), bf16),
        ((2, GROUP, 16, LANES), bf16),
        ((2, GROUP, 16, LANES), bf16),
        ((UNITS, WIDTH), bf16),
        ((UNITS, WIDTH), bf16),
        ((WIDTH, UNITS), bf16),
        ((WIDTH, UNITS), bf16),
        ((UNITS, WIDTH), f32),
        ((WIDTH, UNITS), f32),
        ((TOKENS, HIDDEN), f32),
        ((2, 2, SIDE, SIDE, 32, LANES), bf16),
        ((2, SIDE, SIDE, 32, LANES), bf16),
        ((2, SIDE, SIDE, 32, LANES), bf16),
        ((2, SIDE - 1, SIDE, 32, LANES), bf16),
        ((2, SIDE, 32, LANES), bf16),
        ((2, SIDE - 1, 32, LANES), bf16),
        ((4, 16, LANES), bf16),
        ((3, 16, LANES), bf16),
        ((16, LANES), bf16),
        ((4, 16, LANES), bf16),
        ((4, 16, LANES), bf16),
        ((2, 4, 16, LANES), bf16),
        ((GROUP,) + dense, f32),
        ((GROUP - 1,) + dense, f32),
        (dense, f32),
        ((8,) + dense, f32),
        ((4,) + dense, f32),
    ]
    count = 224
    moe_out, grad_input, grad_up, grad_down, grad_router, grad_dense = pl.pallas_call(
        step_kernel,
        out_shape=[
            jax.ShapeDtypeStruct(tokens.shape, bf16),
            jax.ShapeDtypeStruct(tokens.shape, bf16),
            jax.ShapeDtypeStruct((WIDTH, UNITS), bf16),
            jax.ShapeDtypeStruct((UNITS, WIDTH), bf16),
            jax.ShapeDtypeStruct((128, LANES), f32),
            jax.ShapeDtypeStruct(dense, f32),
        ],
        in_specs=[vmem] * 8,
        out_specs=[vmem] * 6,
        scratch_shapes=[pltpu.VMEM(shape, kind) for shape, kind in scratch]
        + [pltpu.SemaphoreType.DMA((count,)), pltpu.SemaphoreType.DMA((count,))],
        compiler_params=pltpu.CompilerParams(collective_id=0, has_side_effects=True, vmem_limit_bytes=56 << 20),
    )(tokens, cotangent, routes, ln_gain[None], ln_bias[None], router_weight, up_weight[0], down_weight[0])
    return (moe_out, grad_input, grad_up[None], grad_down[None], grad_router, grad_dense[0], grad_dense[1])


def solution(mesh):
    return jax.shard_map(
        on_device,
        mesh=mesh,
        in_specs=(
            P(("dp", "expert"), None),
            P(("dp", "expert"), None),
            P(("dp", "expert"), None),
            P("dp"),
            P("dp"),
            P("dp", None),
            P("expert", None, "dp"),
            P("expert", "dp", None),
        ),
        out_specs=(
            P(("dp", "expert"), None),
            P(("dp", "expert"), None),
            P("expert", None, "dp"),
            P("expert", "dp", None),
            P("dp", None),
            P("dp"),
            P("dp"),
        ),
        check_vma=False,
    )
```

```python
import jax
import jax.numpy as jnp
from jax import lax
from jax.experimental import pallas as pl
from jax.experimental.pallas import tpu as pltpu
from jax.sharding import PartitionSpec as P

SLICES = 8
CAP = 3
SLOTS = 4
SIDE = 4
GROUP = 16
WIDTH = 256
LANES = 128
HIDDEN = 2048
TOKENS = 128
UNITS = 512
ROWS = 48
CHUNK = SIDE * ROWS
MESH = pl.DeviceIdType.MESH

epsilon = 1e-05
root_half = 0.7071067811865476
inv_root_tau = 0.3989422804014327
f32 = jnp.float32
bf16 = jnp.bfloat16


def gelu_parts(hidden):
    normal_cdf = 0.5 * (1.0 + lax.erf(hidden * root_half))
    density = inv_root_tau * jnp.exp(-0.5 * hidden * hidden)
    return (hidden * normal_cdf, normal_cdf + hidden * density)


class Copies:
    def __init__(self, send_sems, recv_sems):
        self.send_sems, self.recv_sems, self.made = send_sems, recv_sems, []

    def start(self, src, dst, device):
        index = len(self.made)
        copy = pltpu.make_async_remote_copy(
            src_ref=src,
            dst_ref=dst,
            send_sem=self.send_sems.at[index],
            recv_sem=self.recv_sems.at[index],
            device_id=device,
            device_id_type=MESH,
        )
        copy.start()
        self.made.append(copy)
        return copy

    def finish(self):
        for copy in self.made:
            copy.wait_send()


def place():
    dp = lax.axis_index("dp")
    ex = lax.axis_index("expert")
    return dp // SIDE, dp % SIDE, ex // 2, ex % 2, dp, ex


def x_partner(step, x, y, ex):
    return (((x + step) % SIDE) * SIDE + y, ex)


def y_partner(step, x, y, ex):
    return (x * SIDE + (y + step) % SIDE, ex)


def product(left, right, left_dim, right_dim):
    return lax.dot_general(left, right, (((left_dim,), (right_dim,)), ((), ())), preferred_element_type=f32)


def iota(shape, dim):
    return lax.broadcasted_iota(jnp.int32, shape, dim)


def one_hot(found):
    return found.astype(f32).astype(bf16)


def message_row(row):
    slot, expert = row & 3, (row >> 2) & 3
    lane_half, k2, blk = (row >> 4) & 1, (row >> 5) & 3, row >> 7
    return (expert * 4 + k2) * 16 + blk * 8 + lane_half * 4 + slot


def packed_row(row, lane_half):
    slot = row & 3
    good = (slot < CAP) & (((row >> 2) & 1) == lane_half)
    return jnp.where(good, ((row >> 3) & 1) * ROWS + (row >> 4) * CAP + slot, -1)


def step_kernel(
    tokens, cot, routes, gain, bias, router, w1, w2,
    moe_out, grad_in, gu_out, gd_out, router_out, gain_out, bias_out,
    normed, block, held, rt, sends, recvs, ag, wx1, wx2, pown, cs, cr, zs, zr, act, gh, slope, part, rs1, mid, rs2,
    hsend, hrecv, gds, gdr, gus, gur, gd_own, gu_own, base,
    lr, lc, l0, l1, l2, l3, l4, l5, l6, l7, fin, nrm, gb, gbr, gb1, gb2, gb3,
    parts_out, parts_in, dot_send, dot_home,
    send_sems, recv_sems,
):
    x, y, z, c, dp, ex = place()
    outer, inner = z // 4, z % 4
    half, near = inner % 2, inner // 2
    me = outer * 4 + near * 2 + c

    def member(step):
        g = (me + step) % GROUP
        return g, (dp, 2 * (4 * (g // 4) + 2 * ((g % 4) // 2) + half) + g % 2)

    others = [member(step) for step in range(1, GROUP)]
    peers = [((dp + step) % GROUP, ex) for step in range(1, GROUP)]
    along_x = [x_partner(step, x, y, ex) for step in range(1, SIDE)]
    along_y = [y_partner(step, x, y, ex) for step in range(1, SIDE)]
    core = (dp, 2 * z + 1 - c)
    beside = (dp, 2 * (z + 2 - 4 * near) + c)
    over = (dp, 2 * (z + 1 - 2 * half) + c)
    along_in = [(dp, 2 * (outer * 4 + (inner + step) % 4) + c) for step in range(1, 4)]
    along_out = [(dp, 2 * ((outer + step) % 4 * 4 + inner) + c) for step in range(1, 4)]
    octet = [(dp, 8 * outer + (2 * inner + c + step) % 8) for step in range(1, 8)]
    far_half = [(dp, 2 * (4 * outer + 2 * k + 1 - half) + d) for k in range(2) for d in range(2)]

    barrier = pltpu.get_barrier_semaphore()
    greeted = [device for _, device in others] + [device for device in peers] + far_half
    for device in greeted:
        pl.semaphore_signal(barrier, inc=1, device_id=device, device_id_type=MESH)

    def norm(rows):
        values = rows.astype(f32)
        centre = values - jnp.mean(values, axis=1, keepdims=True)
        scale = lax.rsqrt(jnp.mean(centre * centre, axis=1, keepdims=True) + epsilon)
        return centre * scale, scale

    square = (TOKENS, TOKENS)
    lane, line = iota(square, 1), iota(square, 0)
    diagonal = (lane == line).astype(f32)
    named = routes[...].astype(f32)
    first, second = (
        jnp.sum(diagonal * named[k:k + 1], axis=1, keepdims=True).astype(jnp.int32) for k in range(2)
    )
    signed = (first == lane).astype(f32) - (second == lane).astype(f32)
    hit_first = (first == (lane >> 2)).astype(f32) * (lane < 16).astype(f32)
    hit_second = (second == (lane >> 2)).astype(f32) * (lane < 16).astype(f32)
    earlier = product(one_hot(line > lane), (hit_first + hit_second).astype(bf16), 1, 0)
    fits = (earlier == (lane & 3).astype(f32)).astype(f32)
    place_first, place_second = (hit_first * fits).astype(bf16), (hit_second * fits).astype(bf16)
    place_all = place_first + place_second
    arrange = (256, 256)
    to_message = one_hot(message_row(iota(arrange, 1)) == iota(arrange, 0))

    def messages(kind, chosen):
        low, high = (
            jnp.concatenate(
                [chosen[:16, LANES * i:LANES * (i + 1)] for k in (0, 8) for i in range(k + 4 * side, k + 4 * side + 4)],
                axis=0,
            )
            for side in range(2)
        )
        stacked = jnp.concatenate(
            [jnp.where(half == 1, high, low), jnp.where(half == 1, low, high)], axis=0
        ).astype(bf16)
        sends[kind] = product(to_message, stacked, 1, 0).astype(bf16).reshape(GROUP, 16, LANES)

    def returned(kind):
        stacked = product(from_message, hrecv[kind].reshape(256, LANES), 1, 0).astype(bf16).astype(f32)
        sides = [stacked[:TOKENS], stacked[TOKENS:]]
        sides = [jnp.where(half == 1, sides[1], sides[0]), jnp.where(half == 1, sides[0], sides[1])]
        rows = jnp.concatenate(
            [sides[side][16 * i:16 * (i + 1)] for k in (0, 4) for side in range(2) for i in range(k, k + 4)], axis=1
        )
        return jnp.concatenate([rows, jnp.zeros((TOKENS - 16, HIDDEN), f32)], axis=0).astype(bf16)

    messages(0, norm(product(place_all, tokens[...], 0, 0)[:16])[0])
    both = (16, LANES)
    edge = jnp.where(iota(both, 0) == 0, gain[...].astype(f32), jnp.where(iota(both, 0) == 1, bias[...].astype(f32), 0.0))
    for side in range(2):
        block[side, 0:64] = router[64 * side:64 * (side + 1)]
        block[side, 64:80] = edge.astype(bf16)
    held[c, dp] = block[c]
    recvs[0, me] = sends[0, me]

    pl.semaphore_wait(barrier, len(greeted))
    copies = Copies(send_sems, recv_sems)
    sent_n = [copies.start(sends.at[0, g], recvs.at[0, me], device) for g, device in others]
    sent_p = [copies.start(block.at[c], held.at[c, dp], peer) for peer in peers]
    got_w1 = copies.start(w1, wx1, over)
    from_message = one_hot(message_row(iota(arrange, 0)) == iota(arrange, 1))
    normed_value, scale_inv = norm(tokens[...])
    normed[...] = normed_value
    parts_out[...] = jnp.zeros_like(parts_out)
    pack = [one_hot(packed_row(iota((2 * ROWS, 256), 1), part_) == iota((2 * ROWS, 256), 0)) for part_ in range(2)]
    unpack = [one_hot(packed_row(iota((256, 2 * ROWS), 0), part_) == iota((256, 2 * ROWS), 1)) for part_ in range(2)]

    def wait_for(found):
        for copy in found:
            copy.wait_recv()

    def place_rows(kind, feature_rows):
        for blk in range(2):
            ag[kind, blk, x, y] = feature_rows[blk].astype(bf16)

    def packed_rows(kind):
        rows = recvs[kind].reshape(256, LANES)
        both_halves = jnp.concatenate([product(pack[0], rows, 1, 0), product(pack[1], rows, 1, 0)], axis=1)
        return [both_halves[:ROWS], both_halves[ROWS:]]

    def gather_first(kind):
        return [copies.start(ag.at[kind, 0, x, y], ag.at[kind, 0, x, y], device) for device in along_y] + [
            copies.start(ag.at[kind, 1, x, y], ag.at[kind, 1, x, y], device) for device in along_x
        ]

    x_left, x_right, y_down, y_up = (x + 3) % SIDE, (x + 1) % SIDE, (y + 3) % SIDE, (y + 1) % SIDE
    pairs = (pl.ds(0, 2), pl.ds(2, 2))

    def at(kind, blk, place_, which):
        return ag.at[kind, 0, place_, pairs[which]] if blk == 0 else ag.at[kind, 1, pairs[which], place_]

    own, before, after = (x, y), (x_left, y_down), (x_right, y_up)
    ahead, back = (along_x[0], along_y[0]), (along_x[2], along_y[2])

    def move(kind, blk, place_, which, device):
        return copies.start(at(kind, blk, place_[blk], which), at(kind, blk, place_[blk], which), device[blk])

    def gather_second(kind):
        one = [move(kind, blk, own, 0, ahead) for blk in range(2)]
        two = [move(kind, blk, own, 1, back) for blk in range(2)]
        rest = [move(kind, blk, own, 1, ahead) for blk in range(2)]
        return one, two, rest + [move(kind, blk, own, 0, back) for blk in range(2)]

    def gather_last(kind, begun):
        one, two, rest = begun
        rest = list(rest)
        for blk in range(2):
            one[blk].wait_recv()
            rest.append(move(kind, blk, before, 0, ahead))
        for blk in range(2):
            two[blk].wait_recv()
            rest.append(move(kind, blk, after, 1, back))
        return rest

    wait_for(sent_p)
    swap_router = copies.start(held.at[c], held.at[c], core)
    edges = [held[c, i, 64:80].astype(f32) for i in range(GROUP)]
    gain_all = jnp.concatenate([edge_rows[0:1] for edge_rows in edges], axis=1)
    bias_all = jnp.concatenate([edge_rows[1:2] for edge_rows in edges], axis=1)
    normal = (normed[...] * gain_all + bias_all).astype(bf16)
    swap_router.wait_recv()
    for block_id in range(GROUP):
        for side in range(2):
            rt[128 * block_id + 64 * side:128 * block_id + 64 * (side + 1)] = held[side, block_id, 0:64]
    logits = product(normal, rt[...], 1, 0)
    gap = jnp.sum(logits * signed, axis=1, keepdims=True)
    gate_first, gate_second = jax.nn.sigmoid(gap), jax.nn.sigmoid(-gap)
    cot_f = cot[...].astype(f32)
    messages(
        1,
        product(place_first, (gate_first * cot_f).astype(bf16), 0, 0)[:16]
        + product(place_second, (gate_second * cot_f).astype(bf16), 0, 0)[:16],
    )
    recvs[1, me] = sends[1, me]
    sent_s = [copies.start(sends.at[1, g], recvs.at[1, me], device) for g, device in others]
    got_w2 = copies.start(w2, wx2, over)

    wait_for(sent_n)
    place_rows(0, packed_rows(0))
    begun_n = gather_first(0)
    wait_for(begun_n)
    second_n = gather_second(0)
    wait_for(sent_s)
    place_rows(1, packed_rows(1))
    begun_s = gather_first(1)
    last_n = gather_last(0, second_n)
    wait_for(begun_s)
    second_s = gather_second(1)
    wait_for(last_n)
    spots = [2 * (4 * near + 2 * (half if blk == 0 else 1 - half) + c) for blk in range(2)]
    for blk in range(2):
        parts = [held[c, spots[blk] + i, 64:80].astype(f32) for i in range(2)]
        gains = jnp.concatenate([parts[0][0:1], parts[1][0:1]], axis=1)
        biases = jnp.concatenate([parts[0][1:2], parts[1][1:2]], axis=1)
        for group in range(SIDE):
            rows = ag[0, blk, group].reshape(CHUNK, WIDTH).astype(f32)
            nrm[blk, group] = (rows * gains + biases).astype(bf16)

    def rows_of(kind, blk, group):
        return nrm[blk, group] if kind == 0 else ag[1, blk, group].reshape(CHUNK, WIDTH)

    def partial_sum(kind, group):
        if kind == 0:
            return product(rows_of(0, 0, group), w1[...], 1, 0) + product(rows_of(0, 1, group), wx1[...], 1, 0)
        return product(rows_of(1, 0, group), w2[...], 1, 1) + product(rows_of(1, 1, group), wx2[...], 1, 1)

    mine = [(x + c) % SIDE, (x + 3 - c) % SIDE]
    theirs = [(x + 1 - c) % SIDE, (x + 2 + c) % SIDE]
    zoned = {}

    def begin(kind):
        crossed = []
        for j in range(2):
            cs[kind, j] = partial_sum(kind, theirs[j]).astype(bf16)
            crossed.append(copies.start(cs.at[kind, j], cr.at[kind, j], core))
        for j in range(2):
            pown[kind, j] = partial_sum(kind, mine[j])
        for j in range(2):
            crossed[j].wait_recv()
            zs[kind, j] = (pown[kind, j] + cr[kind, j].astype(f32)).astype(bf16)
            zoned[kind, j] = copies.start(zs.at[kind, j], zr.at[kind, j], beside)

    def whole(kind, j):
        zoned[kind, j].wait_recv()
        return zs[kind, j].astype(f32) + zr[kind, j].astype(f32)

    ones = jnp.ones((8, WIDTH), bf16)
    sums = ([], [])

    def summed(values):
        return jnp.sum(values, axis=0, keepdims=True)

    def two_rows(gains, biases):
        wide = (8, gains.shape[1])
        return jnp.where(iota(wide, 0) == 0, gains, jnp.where(iota(wide, 0) == 1, biases, 0.0))

    def spread(kind, values_of, weight_a, weight_b, right_dim, groups=tuple(range(SIDE))):
        for group in groups:
            chunk = values_of[group]
            dots = [None] * SIDE
            for blk, weight in ((0, weight_a), (1, weight_b)):
                term = product(chunk, weight[...], 1, right_dim)
                part[kind, blk, group] = term.astype(bf16).reshape(SIDE, ROWS, WIDTH)
                both_rows = term * ag[1 - kind, blk, group].reshape(CHUNK, WIDTH).astype(f32)
                if kind == 0:
                    low_rows = both_rows.astype(bf16)
                    for line_y in range(SIDE):
                        dot = product(ones, low_rows[ROWS * line_y:ROWS * (line_y + 1)], 1, 1)
                        dots[line_y] = dot if dots[line_y] is None else dots[line_y] + dot
                else:
                    gains, biases = summed(both_rows), summed(term)
                    sums[blk].append((gains, biases))
            if kind == 0:
                for line_y in range(SIDE):
                    parts_out[SIDE * group + line_y, :, 0:ROWS] = dots[line_y]

    def reduce_first(kind):
        found = []
        for step in range(1, SIDE):
            found.append(copies.start(part.at[kind, 0, (x + step) % SIDE], rs1.at[kind, 0, step - 1], along_x[step - 1]))
            found.append(copies.start(part.at[kind, 1, :, (y + step) % SIDE], rs1.at[kind, 1, step - 1], along_y[step - 1]))
        return found

    def reduce_second(kind, found):
        wait_for(found)
        for blk in range(2):
            own = part[kind, 0, x] if blk == 0 else part[kind, 1, :, y]
            total = own.astype(f32)
            for step in range(SIDE - 1):
                total = total + rs1[kind, blk, step].astype(f32)
            mid[kind, blk] = total.astype(bf16)
        again = []
        for step in range(1, SIDE):
            again.append(copies.start(mid.at[kind, 0, (y + step) % SIDE], rs2.at[kind, 0, step - 1], along_y[step - 1]))
            again.append(copies.start(mid.at[kind, 1, (x + step) % SIDE], rs2.at[kind, 1, step - 1], along_x[step - 1]))
        return again

    def reduce_last(kind, again):
        wait_for(again)
        ends = []
        for blk in range(2):
            total = mid[kind, blk, y if blk == 0 else x].astype(f32)
            for step in range(SIDE - 1):
                total = total + rs2[kind, blk, step].astype(f32)
            ends.append(total.astype(bf16))
        return ends

    def send_home(kind, ends):
        rows = jnp.concatenate(ends, axis=0)
        out = product(unpack[0], rows[:, :LANES], 1, 0) + product(unpack[1], rows[:, LANES:], 1, 0)
        hsend[kind] = out.astype(bf16).reshape(GROUP, 16, LANES)
        hrecv[kind, me] = hsend[kind, me]
        return [copies.start(hsend.at[kind, g], hrecv.at[kind, me], device) for g, device in others]

    got_w1.wait_recv()
    begin(0)
    wait_for(gather_last(1, second_s))
    got_w2.wait_recv()
    begin(1)
    shared = []
    for j in range(2):
        value, grade = gelu_parts(whole(0, j))
        act[mine[j]] = value.astype(bf16)
        shared.append(copies.start(act.at[mine[j]], act.at[mine[j]], core))
        slope[j] = grade
    wait_for(shared)
    spread(0, act, w2, wx2, 0)
    sent_d = [
        copies.start(parts_out.at[(dp + step) % GROUP], parts_in.at[step - 1], peer) for step, peer in enumerate(peers, 1)
    ]
    found_out = reduce_first(0)
    active = act[...].reshape(SIDE * CHUNK, UNITS)
    gds[...] = product(active, ag[1, 1].reshape(SIDE * CHUNK, WIDTH), 0, 0).astype(bf16)
    got_gd = copies.start(gds, gdr, over)
    gd_own[...] = product(active, ag[1, 0].reshape(SIDE * CHUNK, WIDTH), 0, 0)

    wait_for(sent_d)
    total = parts_out[dp]
    for step in range(GROUP - 1):
        total = total + parts_in[step]
    dot_send[...] = total
    dot_home[me] = total
    sent_d = [copies.start(dot_send, dot_home.at[me], device) for _, device in others]
    shared = []
    for j in range(2):
        gh[mine[j]] = (whole(1, j) * slope[j]).astype(bf16)
        shared.append(copies.start(gh.at[mine[j]], gh.at[mine[j]], core))
        spread(1, gh, w1, wx1, 1, (mine[j],))
    for j in range(2):
        shared[j].wait_recv()
        spread(1, gh, w1, wx1, 1, (theirs[j],))
    found_in = reduce_first(1)
    again_out = reduce_second(0, found_out)
    grads = gh[...].reshape(SIDE * CHUNK, UNITS)
    gus[...] = product(nrm[1].reshape(SIDE * CHUNK, WIDTH), grads, 0, 0).astype(bf16)
    got_gu = copies.start(gus, gur, over)
    gu_own[...] = product(nrm[0].reshape(SIDE * CHUNK, WIDTH), grads, 0, 0)

    wait_for(sent_d)
    dots = jnp.zeros((8, LANES), f32)
    for expert in range(4):
        total = (dot_home[4 * expert] + dot_home[4 * expert + 1]) + (dot_home[4 * expert + 2] + dot_home[4 * expert + 3])
        dots = dots + jnp.where(iota((8, LANES), 0) == expert, total, 0.0)
    chooser = one_hot((line == me * CAP + (lane & 3)) & ((lane & 3) < CAP))
    dots_high = dots.astype(bf16)
    dots_low = (dots - dots_high.astype(f32)).astype(bf16)
    chosen = product(dots_high, chooser, 1, 0) + product(dots_low, chooser, 1, 0)
    chosen = summed(jnp.where(iota((8, LANES), 0) == (iota((8, LANES), 1) >> 2), chosen, 0.0))
    dot_first = jnp.sum(place_first.astype(f32) * chosen, axis=1, keepdims=True)
    dot_second = jnp.sum(place_second.astype(f32) * chosen, axis=1, keepdims=True)
    gap_grad = dot_first * gate_second - dot_second * gate_first
    normal = (normed[...] * gain_all + bias_all).astype(bf16)
    local = product(normal, (gap_grad * signed).astype(bf16), 0, 0).astype(bf16)
    for block_id in range(GROUP):
        for side in range(2):
            for path in range(2):
                begin_row = 128 * block_id + 64 * side + 32 * path
                lr[side, path, block_id // SIDE, block_id % SIDE] = local[begin_row:begin_row + 32]
    cored = copies.start(lr.at[1 - c], lc, core)

    base_value = gap_grad * product(signed.astype(bf16), rt[...], 1, 1)
    base[...] = base_value
    dense = two_rows(summed(base_value * normed[...]), summed(base_value))
    for block_id in range(GROUP):
        gb[block_id] = dense[:, 128 * block_id:128 * (block_id + 1)]
    for blk in range(2):
        gains = sum(pair_[0] for pair_ in sums[blk])
        biases = sum(pair_[1] for pair_ in sums[blk])
        dense = two_rows(gains, biases)
        for i in range(2):
            gb[spots[blk] + i] = gb[spots[blk] + i] + dense[:, LANES * i:LANES * (i + 1)]
    cored.wait_recv()
    l0[...] = (lr[c].astype(f32) + lc[...].astype(f32)).astype(bf16)
    sent_l = []
    for step in range(1, SIDE):
        sent_l.append(copies.start(l0.at[0, (x + step) % SIDE], l1.at[0, step - 1], along_x[step - 1]))
        sent_l.append(copies.start(l0.at[1, :, (y + step) % SIDE], l1.at[1, step - 1], along_y[step - 1]))
    sent_g = [
        copies.start(gb.at[(dp + step) % GROUP], gbr.at[step - 1], peer) for step, peer in enumerate(peers, 1)
    ]
    again_in = reduce_second(1, found_in)
    home_out = send_home(0, reduce_last(0, again_out))
    wait_for(sent_l)
    for path in range(2):
        own_part = l0[0, x] if path == 0 else l0[1, :, y]
        l2[path] = (
            own_part.astype(f32) + l1[path, 0].astype(f32) + l1[path, 1].astype(f32) + l1[path, 2].astype(f32)
        ).astype(bf16)
    sent_l = []
    for step in range(1, SIDE):
        sent_l.append(copies.start(l2.at[0, (y + step) % SIDE], l3.at[0, step - 1], along_y[step - 1]))
        sent_l.append(copies.start(l2.at[1, (x + step) % SIDE], l3.at[1, step - 1], along_x[step - 1]))
    home_in = send_home(1, reduce_last(1, again_in))
    wait_for(sent_g)
    total = gb[dp]
    for step in range(GROUP - 1):
        total = total + gbr[step]
    gb1[...] = total
    gb2[2 * inner + c] = total
    sent_g = [copies.start(gb1, gb2.at[2 * inner + c], device) for device in octet]
    wait_for(sent_l)
    for path in range(2):
        own_part = l2[path, y if path == 0 else x]
        total = (own_part.astype(f32) + l3[path, 0].astype(f32)) + (l3[path, 1].astype(f32) + l3[path, 2].astype(f32))
        l4[2 * path] = total[0:16].astype(bf16)
        l4[2 * path + 1] = total[16:32].astype(bf16)
    sent_l = [copies.start(l4.at[(inner + step) % 4], l5.at[step - 1], along_in[step - 1]) for step in range(1, 4)]
    wait_for(sent_g)
    total = gb2[0]
    for i in range(1, 8):
        total = total + gb2[i]
    gb3[outer] = total
    sent_g = [copies.start(gb3.at[outer], gb3.at[outer], device) for device in along_out]
    wait_for(sent_l)
    l6[...] = (
        (l4[inner].astype(f32) + l5[0].astype(f32)) + (l5[1].astype(f32) + l5[2].astype(f32))
    ).astype(bf16)
    sent_l = [copies.start(l6, l7.at[outer], device) for device in along_out]
    l7[outer] = l6[...]

    wait_for(home_out)
    rows = returned(0)
    moe_out[...] = (
        gate_first * product(place_first, rows, 1, 0) + gate_second * product(place_second, rows, 1, 0)
    ).astype(bf16)
    wait_for(home_in)
    grad_norm = (product(place_all, returned(1), 1, 0) + base[...]) * gain_all
    mean_grad = jnp.mean(grad_norm, axis=1, keepdims=True)
    mean_both = jnp.mean(grad_norm * normed[...], axis=1, keepdims=True)
    grad_in[...] = (scale_inv * (grad_norm - mean_grad - normed[...] * mean_both)).astype(bf16)
    wait_for(sent_l)
    fin[c, inner] = (
        (l7[0].astype(f32) + l7[1].astype(f32)) + (l7[2].astype(f32) + l7[3].astype(f32))
    ).astype(bf16)
    sent_l = [copies.start(fin.at[c, inner], fin.at[c, inner], device) for device in octet]
    got_gd.wait_recv()
    gd_out[...] = (gd_own[...] + gdr[...].astype(f32)).astype(bf16)
    got_gu.wait_recv()
    gu_out[...] = (gu_own[...] + gur[...].astype(f32)).astype(bf16)
    wait_for(sent_g)
    total = (gb3[0] + gb3[1]) + (gb3[2] + gb3[3])
    gain_out[...] = total[0:1]
    bias_out[...] = total[1:2]
    wait_for(sent_l)
    router_out[...] = fin[...].astype(f32).reshape(128, 128)
    copies.finish()


def last_kernel(*refs):
    count = len(refs) // 2
    for i in range(count):
        refs[count + i][...] = refs[i][...]


def on_device(tokens, cotangent, routes, ln_gain, ln_bias, router_weight, up_weight, down_weight):
    vmem = pl.BlockSpec(memory_space=pltpu.VMEM)
    pair = (2, 2, CHUNK, UNITS)
    moved = (2, 2, SIDE, SIDE, ROWS, WIDTH)
    dense = (8, LANES)
    scratch = [
        ((TOKENS, HIDDEN), f32),
        ((2, 80, LANES), bf16),
        ((2, GROUP, 80, LANES), bf16),
        ((HIDDEN, LANES), bf16),
        ((2, GROUP, 16, LANES), bf16),
        ((2, GROUP, 16, LANES), bf16),
        (moved, bf16),
        ((WIDTH, UNITS), bf16),
        ((UNITS, WIDTH), bf16),
        (pair, f32),
        (pair, bf16),
        (pair, bf16),
        (pair, bf16),
        (pair, bf16),
        ((SIDE, CHUNK, UNITS), bf16),
        ((SIDE, CHUNK, UNITS), bf16),
        ((2, CHUNK, UNITS), f32),
        (moved, bf16),
        ((2, 2, SIDE - 1, SIDE, ROWS, WIDTH), bf16),
        ((2, 2, SIDE, ROWS, WIDTH), bf16),
        ((2, 2, SIDE - 1, ROWS, WIDTH), bf16),
        ((2, GROUP, 16, LANES), bf16),
        ((2, GROUP, 16, LANES), bf16),
        ((UNITS, WIDTH), bf16),
        ((UNITS, WIDTH), bf16),
        ((WIDTH, UNITS), bf16),
        ((WIDTH, UNITS), bf16),
        ((UNITS, WIDTH), f32),
        ((WIDTH, UNITS), f32),
        ((TOKENS, HIDDEN), f32),
        ((2, 2, SIDE, SIDE, 32, LANES), bf16),
        ((2, SIDE, SIDE, 32, LANES), bf16),
        ((2, SIDE, SIDE, 32, LANES), bf16),
        ((2, SIDE - 1, SIDE, 32, LANES), bf16),
        ((2, SIDE, 32, LANES), bf16),
        ((2, SIDE - 1, 32, LANES), bf16),
        ((4, 16, LANES), bf16),
        ((3, 16, LANES), bf16),
        ((16, LANES), bf16),
        ((4, 16, LANES), bf16),
        ((2, 4, 16, LANES), bf16),
        ((2, SIDE, CHUNK, WIDTH), bf16),
        ((GROUP,) + dense, f32),
        ((GROUP - 1,) + dense, f32),
        (dense, f32),
        ((8,) + dense, f32),
        ((4,) + dense, f32),
        ((GROUP,) + dense, f32),
        ((GROUP - 1,) + dense, f32),
        (dense, f32),
        ((GROUP,) + dense, f32),
    ]
    count = 256
    found = pl.pallas_call(
        step_kernel,
        out_shape=[
            jax.ShapeDtypeStruct(tokens.shape, bf16),
            jax.ShapeDtypeStruct(tokens.shape, bf16),
            jax.ShapeDtypeStruct((WIDTH, UNITS), bf16),
            jax.ShapeDtypeStruct((UNITS, WIDTH), bf16),
            jax.ShapeDtypeStruct((128, LANES), f32),
            jax.ShapeDtypeStruct((1, LANES), f32),
            jax.ShapeDtypeStruct((1, LANES), f32),
        ],
        in_specs=[vmem] * 8,
        out_specs=[vmem] * 7,
        scratch_shapes=[pltpu.VMEM(shape, kind) for shape, kind in scratch]
        + [pltpu.SemaphoreType.DMA((count,)), pltpu.SemaphoreType.DMA((count,))],
        compiler_params=pltpu.CompilerParams(collective_id=0, has_side_effects=True, vmem_limit_bytes=56 << 20),
    )(tokens, cotangent, routes.T, ln_gain[None], ln_bias[None], router_weight, up_weight[0], down_weight[0])
    moe_out, grad_input, grad_up, grad_down, grad_router, grad_gain, grad_bias = pl.pallas_call(
        last_kernel,
        out_shape=[jax.ShapeDtypeStruct(array.shape, array.dtype) for array in found],
        in_specs=[vmem] * 7,
        out_specs=[vmem] * 7,
        compiler_params=pltpu.CompilerParams(vmem_limit_bytes=60 << 20),
    )(*found)
    return (moe_out, grad_input, grad_up[None], grad_down[None], grad_router, grad_gain[0], grad_bias[0])


def solution(mesh):
    return jax.shard_map(
        on_device,
        mesh=mesh,
        in_specs=(
            P(("dp", "expert"), None),
            P(("dp", "expert"), None),
            P(("dp", "expert"), None),
            P("dp"),
            P("dp"),
            P("dp", None),
            P("expert", None, "dp"),
            P("expert", "dp", None),
        ),
        out_specs=(
            P(("dp", "expert"), None),
            P(("dp", "expert"), None),
            P("expert", None, "dp"),
            P("expert", "dp", None),
            P("dp", None),
            P("dp"),
            P("dp"),
        ),
        check_vma=False,
    )
```

```python
import jax
import jax.numpy as jnp
from jax import lax
from jax.experimental import pallas as pl
from jax.experimental.pallas import tpu as pltpu
from jax.sharding import PartitionSpec as P

SLICES = 8
CAP = 3
SLOTS = 4
SIDE = 4
GROUP = 16
WIDTH = 256
LANES = 128
HIDDEN = 2048
TOKENS = 128
UNITS = 512
ROWS = 48
CHUNK = SIDE * ROWS
MESH = pl.DeviceIdType.MESH

epsilon = 1e-05
root_half = 0.7071067811865476
inv_root_tau = 0.3989422804014327
f32 = jnp.float32
bf16 = jnp.bfloat16


def gelu_parts(hidden):
    normal_cdf = 0.5 * (1.0 + lax.erf(hidden * root_half))
    density = inv_root_tau * jnp.exp(-0.5 * hidden * hidden)
    return (hidden * normal_cdf, normal_cdf + hidden * density)


class Copies:
    def __init__(self, send_sems, recv_sems):
        self.send_sems, self.recv_sems, self.made = send_sems, recv_sems, []

    def start(self, src, dst, device):
        index = len(self.made)
        copy = pltpu.make_async_remote_copy(
            src_ref=src,
            dst_ref=dst,
            send_sem=self.send_sems.at[index],
            recv_sem=self.recv_sems.at[index],
            device_id=device,
            device_id_type=MESH,
        )
        copy.start()
        self.made.append(copy)
        return copy

    def finish(self):
        for copy in self.made:
            copy.wait_send()


def place():
    dp = lax.axis_index("dp")
    ex = lax.axis_index("expert")
    return dp // SIDE, dp % SIDE, ex // 2, ex % 2, dp, ex


def x_partner(step, x, y, ex):
    return (((x + step) % SIDE) * SIDE + y, ex)


def y_partner(step, x, y, ex):
    return (x * SIDE + (y + step) % SIDE, ex)


def product(left, right, left_dim, right_dim):
    return lax.dot_general(left, right, (((left_dim,), (right_dim,)), ((), ())), preferred_element_type=f32)


def iota(shape, dim):
    return lax.broadcasted_iota(jnp.int32, shape, dim)


def one_hot(found):
    return found.astype(f32).astype(bf16)


def message_row(row):
    slot, expert = row & 3, (row >> 2) & 3
    lane_half, k2, blk = (row >> 4) & 1, (row >> 5) & 3, row >> 7
    return (expert * 4 + k2) * 16 + blk * 8 + lane_half * 4 + slot


def packed_row(row, lane_half):
    slot = row & 3
    good = (slot < CAP) & (((row >> 2) & 1) == lane_half)
    return jnp.where(good, ((row >> 3) & 1) * ROWS + (row >> 4) * CAP + slot, -1)


def step_kernel(
    tokens, cot, routes, gain, bias, router, w1, w2,
    moe_out, grad_in, gu_out, gd_out, router_out, gain_out, bias_out,
    normed, block, held, rt, sends, recvs, ag, wx1, wx2, pown, cs, cr, zs, zr, act, gh, slope, part, rs1, mid, rs2,
    hsend, hrecv, gds, gdr, gus, gur, gd_own, gu_own, base,
    lr, lc, l0, l1, l2, l3, l4, l5, l6, l7, fin, nrm, gb, gbr, gb1, gb2, gb3,
    parts_out, parts_in, dot_send, dot_home,
    send_sems, recv_sems,
):
    x, y, z, c, dp, ex = place()
    outer, inner = z // 4, z % 4
    half, near = inner % 2, inner // 2
    me = outer * 4 + near * 2 + c

    def member(step):
        g = (me + step) % GROUP
        return g, (dp, 2 * (4 * (g // 4) + 2 * ((g % 4) // 2) + half) + g % 2)

    others = [member(step) for step in range(1, GROUP)]
    peers = [((dp + step) % GROUP, ex) for step in range(1, GROUP)]
    along_x = [x_partner(step, x, y, ex) for step in range(1, SIDE)]
    along_y = [y_partner(step, x, y, ex) for step in range(1, SIDE)]
    core = (dp, 2 * z + 1 - c)
    beside = (dp, 2 * (z + 2 - 4 * near) + c)
    over = (dp, 2 * (z + 1 - 2 * half) + c)
    along_in = [(dp, 2 * (outer * 4 + (inner + step) % 4) + c) for step in range(1, 4)]
    along_out = [(dp, 2 * ((outer + step) % 4 * 4 + inner) + c) for step in range(1, 4)]
    octet = [(dp, 8 * outer + (2 * inner + c + step) % 8) for step in range(1, 8)]
    far_half = [(dp, 2 * (4 * outer + 2 * k + 1 - half) + d) for k in range(2) for d in range(2)]

    barrier = pltpu.get_barrier_semaphore()
    greeted = [device for _, device in others] + [device for device in peers] + far_half
    for device in greeted:
        pl.semaphore_signal(barrier, inc=1, device_id=device, device_id_type=MESH)

    def norm(rows):
        values = rows.astype(f32)
        centre = values - jnp.mean(values, axis=1, keepdims=True)
        scale = lax.rsqrt(jnp.mean(centre * centre, axis=1, keepdims=True) + epsilon)
        return centre * scale, scale

    square = (TOKENS, TOKENS)
    lane, line = iota(square, 1), iota(square, 0)
    diagonal = (lane == line).astype(f32)
    named = routes[...].astype(f32)
    first, second = (
        jnp.sum(diagonal * named[k:k + 1], axis=1, keepdims=True).astype(jnp.int32) for k in range(2)
    )
    signed = (first == lane).astype(f32) - (second == lane).astype(f32)
    hit_first = (first == (lane >> 2)).astype(f32) * (lane < 16).astype(f32)
    hit_second = (second == (lane >> 2)).astype(f32) * (lane < 16).astype(f32)
    earlier = product(one_hot(line > lane), (hit_first + hit_second).astype(bf16), 1, 0)
    fits = (earlier == (lane & 3).astype(f32)).astype(f32)
    place_first, place_second = (hit_first * fits).astype(bf16), (hit_second * fits).astype(bf16)
    place_all = place_first + place_second
    arrange = (256, 256)
    to_message = one_hot(message_row(iota(arrange, 1)) == iota(arrange, 0))

    def messages(kind, chosen):
        low, high = (
            jnp.concatenate(
                [chosen[:16, LANES * i:LANES * (i + 1)] for k in (0, 8) for i in range(k + 4 * side, k + 4 * side + 4)],
                axis=0,
            )
            for side in range(2)
        )
        stacked = jnp.concatenate(
            [jnp.where(half == 1, high, low), jnp.where(half == 1, low, high)], axis=0
        ).astype(bf16)
        sends[kind] = product(to_message, stacked, 1, 0).astype(bf16).reshape(GROUP, 16, LANES)

    def returned(kind):
        stacked = product(from_message, hrecv[kind].reshape(256, LANES), 1, 0).astype(bf16).astype(f32)
        sides = [stacked[:TOKENS], stacked[TOKENS:]]
        sides = [jnp.where(half == 1, sides[1], sides[0]), jnp.where(half == 1, sides[0], sides[1])]
        rows = jnp.concatenate(
            [sides[side][16 * i:16 * (i + 1)] for k in (0, 4) for side in range(2) for i in range(k, k + 4)], axis=1
        )
        return jnp.concatenate([rows, jnp.zeros((TOKENS - 16, HIDDEN), f32)], axis=0).astype(bf16)

    messages(0, norm(product(place_all, tokens[...], 0, 0)[:16])[0])
    both = (16, LANES)
    edge = jnp.where(iota(both, 0) == 0, gain[...].astype(f32), jnp.where(iota(both, 0) == 1, bias[...].astype(f32), 0.0))
    for side in range(2):
        block[side, 0:64] = router[64 * side:64 * (side + 1)]
        block[side, 64:80] = edge.astype(bf16)
    held[c, dp] = block[c]
    recvs[0, me] = sends[0, me]

    pl.semaphore_wait(barrier, len(greeted))
    copies = Copies(send_sems, recv_sems)
    sent_n = [copies.start(sends.at[0, g], recvs.at[0, me], device) for g, device in others]
    sent_p = [copies.start(block.at[c], held.at[c, dp], peer) for peer in peers]
    got_w1 = copies.start(w1, wx1, over)
    from_message = one_hot(message_row(iota(arrange, 0)) == iota(arrange, 1))
    normed_value, scale_inv = norm(tokens[...])
    normed[...] = normed_value
    parts_out[...] = jnp.zeros_like(parts_out)
    pack = [one_hot(packed_row(iota((2 * ROWS, 256), 1), part_) == iota((2 * ROWS, 256), 0)) for part_ in range(2)]
    unpack = [one_hot(packed_row(iota((256, 2 * ROWS), 0), part_) == iota((256, 2 * ROWS), 1)) for part_ in range(2)]

    def wait_for(found):
        for copy in found:
            copy.wait_recv()

    def place_rows(kind, feature_rows):
        for blk in range(2):
            ag[kind, blk, x, y] = feature_rows[blk].astype(bf16)

    def packed_rows(kind):
        rows = recvs[kind].reshape(256, LANES)
        both_halves = jnp.concatenate([product(pack[0], rows, 1, 0), product(pack[1], rows, 1, 0)], axis=1)
        return [both_halves[:ROWS], both_halves[ROWS:]]

    def gather_first(kind):
        return [copies.start(ag.at[kind, 0, x, y], ag.at[kind, 0, x, y], device) for device in along_y] + [
            copies.start(ag.at[kind, 1, x, y], ag.at[kind, 1, x, y], device) for device in along_x
        ]

    x_left, x_right, y_down, y_up = (x + 3) % SIDE, (x + 1) % SIDE, (y + 3) % SIDE, (y + 1) % SIDE
    pairs = (pl.ds(0, 2), pl.ds(2, 2))

    def at(kind, blk, place_, which):
        return ag.at[kind, 0, place_, pairs[which]] if blk == 0 else ag.at[kind, 1, pairs[which], place_]

    own, before, after = (x, y), (x_left, y_down), (x_right, y_up)
    ahead, back = (along_x[0], along_y[0]), (along_x[2], along_y[2])

    def move(kind, blk, place_, which, device):
        return copies.start(at(kind, blk, place_[blk], which), at(kind, blk, place_[blk], which), device[blk])

    def gather_second(kind):
        one = [move(kind, blk, own, 0, ahead) for blk in range(2)]
        two = [move(kind, blk, own, 1, back) for blk in range(2)]
        rest = [move(kind, blk, own, 1, ahead) for blk in range(2)]
        return one, two, rest + [move(kind, blk, own, 0, back) for blk in range(2)]

    def gather_last(kind, begun):
        one, two, rest = begun
        rest = list(rest)
        for blk in range(2):
            one[blk].wait_recv()
            rest.append(move(kind, blk, before, 0, ahead))
        for blk in range(2):
            two[blk].wait_recv()
            rest.append(move(kind, blk, after, 1, back))
        return rest

    wait_for(sent_p)
    swap_router = copies.start(held.at[c], held.at[c], core)
    edges = [held[c, i, 64:80].astype(f32) for i in range(GROUP)]
    gain_all = jnp.concatenate([edge_rows[0:1] for edge_rows in edges], axis=1)
    bias_all = jnp.concatenate([edge_rows[1:2] for edge_rows in edges], axis=1)
    normal = (normed[...] * gain_all + bias_all).astype(bf16)
    swap_router.wait_recv()
    for block_id in range(GROUP):
        for side in range(2):
            rt[128 * block_id + 64 * side:128 * block_id + 64 * (side + 1)] = held[side, block_id, 0:64]
    logits = product(normal, rt[...], 1, 0)
    gap = jnp.sum(logits * signed, axis=1, keepdims=True)
    gate_first, gate_second = jax.nn.sigmoid(gap), jax.nn.sigmoid(-gap)
    cot_f = cot[...].astype(f32)
    messages(
        1,
        product(place_first, (gate_first * cot_f).astype(bf16), 0, 0)[:16]
        + product(place_second, (gate_second * cot_f).astype(bf16), 0, 0)[:16],
    )
    recvs[1, me] = sends[1, me]
    sent_s = [copies.start(sends.at[1, g], recvs.at[1, me], device) for g, device in others]
    got_w2 = copies.start(w2, wx2, over)

    wait_for(sent_n)
    place_rows(0, packed_rows(0))
    begun_n = gather_first(0)
    wait_for(begun_n)
    second_n = gather_second(0)
    wait_for(sent_s)
    place_rows(1, packed_rows(1))
    begun_s = gather_first(1)
    last_n = gather_last(0, second_n)
    wait_for(begun_s)
    second_s = gather_second(1)
    wait_for(last_n)
    spots = [2 * (4 * near + 2 * (half if blk == 0 else 1 - half) + c) for blk in range(2)]
    for blk in range(2):
        parts = [held[c, spots[blk] + i, 64:80].astype(f32) for i in range(2)]
        gains = jnp.concatenate([parts[0][0:1], parts[1][0:1]], axis=1)
        biases = jnp.concatenate([parts[0][1:2], parts[1][1:2]], axis=1)
        for group in range(SIDE):
            rows = ag[0, blk, group].reshape(CHUNK, WIDTH).astype(f32)
            nrm[blk, group] = (rows * gains + biases).astype(bf16)

    def rows_of(kind, blk, group):
        return nrm[blk, group] if kind == 0 else ag[1, blk, group].reshape(CHUNK, WIDTH)

    def partial_sum(kind, group):
        if kind == 0:
            return product(rows_of(0, 0, group), w1[...], 1, 0) + product(rows_of(0, 1, group), wx1[...], 1, 0)
        return product(rows_of(1, 0, group), w2[...], 1, 1) + product(rows_of(1, 1, group), wx2[...], 1, 1)

    mine = [(x + c) % SIDE, (x + 3 - c) % SIDE]
    theirs = [(x + 1 - c) % SIDE, (x + 2 + c) % SIDE]
    zoned = {}

    def begin(kind):
        crossed = []
        for j in range(2):
            cs[kind, j] = partial_sum(kind, theirs[j]).astype(bf16)
            crossed.append(copies.start(cs.at[kind, j], cr.at[kind, j], core))
        for j in range(2):
            pown[kind, j] = partial_sum(kind, mine[j])
        for j in range(2):
            crossed[j].wait_recv()
            zs[kind, j] = (pown[kind, j] + cr[kind, j].astype(f32)).astype(bf16)
            zoned[kind, j] = copies.start(zs.at[kind, j], zr.at[kind, j], beside)

    def whole(kind, j):
        zoned[kind, j].wait_recv()
        return zs[kind, j].astype(f32) + zr[kind, j].astype(f32)

    ones = jnp.ones((8, WIDTH), bf16)
    sums = ([], [])

    def summed(values):
        return jnp.sum(values, axis=0, keepdims=True)

    def two_rows(gains, biases):
        wide = (8, gains.shape[1])
        return jnp.where(iota(wide, 0) == 0, gains, jnp.where(iota(wide, 0) == 1, biases, 0.0))

    def spread(kind, values_of, weight_a, weight_b, right_dim, groups=tuple(range(SIDE))):
        for group in groups:
            chunk = values_of[group]
            dots = [None] * SIDE
            for blk, weight in ((0, weight_a), (1, weight_b)):
                term = product(chunk, weight[...], 1, right_dim)
                part[kind, blk, group] = term.astype(bf16).reshape(SIDE, ROWS, WIDTH)
                both_rows = term * ag[1 - kind, blk, group].reshape(CHUNK, WIDTH).astype(f32)
                if kind == 0:
                    low_rows = both_rows.astype(bf16)
                    for line_y in range(SIDE):
                        dot = product(ones, low_rows[ROWS * line_y:ROWS * (line_y + 1)], 1, 1)
                        dots[line_y] = dot if dots[line_y] is None else dots[line_y] + dot
                else:
                    gains, biases = summed(both_rows), summed(term)
                    sums[blk].append((gains, biases))
            if kind == 0:
                for line_y in range(SIDE):
                    parts_out[SIDE * group + line_y, :, 0:ROWS] = dots[line_y]

    def reduce_first(kind):
        found = []
        for step in range(1, SIDE):
            found.append(copies.start(part.at[kind, 0, (x + step) % SIDE], rs1.at[kind, 0, step - 1], along_x[step - 1]))
            found.append(copies.start(part.at[kind, 1, :, (y + step) % SIDE], rs1.at[kind, 1, step - 1], along_y[step - 1]))
        return found

    def reduce_second(kind, found):
        wait_for(found)
        for blk in range(2):
            own = part[kind, 0, x] if blk == 0 else part[kind, 1, :, y]
            total = own.astype(f32)
            for step in range(SIDE - 1):
                total = total + rs1[kind, blk, step].astype(f32)
            mid[kind, blk] = total.astype(bf16)
        again = []
        for step in range(1, SIDE):
            again.append(copies.start(mid.at[kind, 0, (y + step) % SIDE], rs2.at[kind, 0, step - 1], along_y[step - 1]))
            again.append(copies.start(mid.at[kind, 1, (x + step) % SIDE], rs2.at[kind, 1, step - 1], along_x[step - 1]))
        return again

    def reduce_last(kind, again):
        wait_for(again)
        ends = []
        for blk in range(2):
            total = mid[kind, blk, y if blk == 0 else x].astype(f32)
            for step in range(SIDE - 1):
                total = total + rs2[kind, blk, step].astype(f32)
            ends.append(total.astype(bf16))
        return ends

    def send_home(kind, ends):
        rows = jnp.concatenate(ends, axis=0)
        out = product(unpack[0], rows[:, :LANES], 1, 0) + product(unpack[1], rows[:, LANES:], 1, 0)
        hsend[kind] = out.astype(bf16).reshape(GROUP, 16, LANES)
        hrecv[kind, me] = hsend[kind, me]
        return [copies.start(hsend.at[kind, g], hrecv.at[kind, me], device) for g, device in others]

    got_w1.wait_recv()
    begin(0)
    wait_for(gather_last(1, second_s))
    got_w2.wait_recv()
    begin(1)
    shared = []
    for j in range(2):
        value, grade = gelu_parts(whole(0, j))
        act[mine[j]] = value.astype(bf16)
        shared.append(copies.start(act.at[mine[j]], act.at[mine[j]], core))
        slope[j] = grade
    wait_for(shared)
    spread(0, act, w2, wx2, 0)
    sent_d = [
        copies.start(parts_out.at[(dp + step) % GROUP], parts_in.at[step - 1], peer) for step, peer in enumerate(peers, 1)
    ]
    found_out = reduce_first(0)
    active = act[...].reshape(SIDE * CHUNK, UNITS)
    gds[...] = product(active, ag[1, 1].reshape(SIDE * CHUNK, WIDTH), 0, 0).astype(bf16)
    gd_own[...] = product(active, ag[1, 0].reshape(SIDE * CHUNK, WIDTH), 0, 0)

    wait_for(sent_d)
    total = parts_out[dp]
    for step in range(GROUP - 1):
        total = total + parts_in[step]
    dot_send[...] = total
    dot_home[me] = total
    sent_d = [copies.start(dot_send, dot_home.at[me], device) for _, device in others]
    shared = []
    for j in range(2):
        gh[mine[j]] = (whole(1, j) * slope[j]).astype(bf16)
        shared.append(copies.start(gh.at[mine[j]], gh.at[mine[j]], core))
        spread(1, gh, w1, wx1, 1, (mine[j],))
    got_gd = copies.start(gds, gdr, over)
    for j in range(2):
        shared[j].wait_recv()
        spread(1, gh, w1, wx1, 1, (theirs[j],))
    found_in = reduce_first(1)
    again_out = reduce_second(0, found_out)
    grads = gh[...].reshape(SIDE * CHUNK, UNITS)
    gus[...] = product(nrm[1].reshape(SIDE * CHUNK, WIDTH), grads, 0, 0).astype(bf16)
    got_gu = copies.start(gus, gur, over)
    gu_own[...] = product(nrm[0].reshape(SIDE * CHUNK, WIDTH), grads, 0, 0)

    wait_for(sent_d)
    dots = jnp.zeros((8, LANES), f32)
    for expert in range(4):
        total = (dot_home[4 * expert] + dot_home[4 * expert + 1]) + (dot_home[4 * expert + 2] + dot_home[4 * expert + 3])
        dots = dots + jnp.where(iota((8, LANES), 0) == expert, total, 0.0)
    chooser = one_hot((line == me * CAP + (lane & 3)) & ((lane & 3) < CAP))
    dots_high = dots.astype(bf16)
    dots_low = (dots - dots_high.astype(f32)).astype(bf16)
    chosen = product(dots_high, chooser, 1, 0) + product(dots_low, chooser, 1, 0)
    chosen = summed(jnp.where(iota((8, LANES), 0) == (iota((8, LANES), 1) >> 2), chosen, 0.0))
    dot_first = jnp.sum(place_first.astype(f32) * chosen, axis=1, keepdims=True)
    dot_second = jnp.sum(place_second.astype(f32) * chosen, axis=1, keepdims=True)
    gap_grad = dot_first * gate_second - dot_second * gate_first
    normal = (normed[...] * gain_all + bias_all).astype(bf16)
    local = product(normal, (gap_grad * signed).astype(bf16), 0, 0).astype(bf16)
    for block_id in range(GROUP):
        for side in range(2):
            for path in range(2):
                begin_row = 128 * block_id + 64 * side + 32 * path
                lr[side, path, block_id // SIDE, block_id % SIDE] = local[begin_row:begin_row + 32]
    cored = copies.start(lr.at[1 - c], lc, core)

    base_value = gap_grad * product(signed.astype(bf16), rt[...], 1, 1)
    base[...] = base_value
    dense = two_rows(summed(base_value * normed[...]), summed(base_value))
    for block_id in range(GROUP):
        gb[block_id] = dense[:, 128 * block_id:128 * (block_id + 1)]
    for blk in range(2):
        gains = sum(pair_[0] for pair_ in sums[blk])
        biases = sum(pair_[1] for pair_ in sums[blk])
        dense = two_rows(gains, biases)
        for i in range(2):
            gb[spots[blk] + i] = gb[spots[blk] + i] + dense[:, LANES * i:LANES * (i + 1)]
    cored.wait_recv()
    l0[...] = (lr[c].astype(f32) + lc[...].astype(f32)).astype(bf16)
    sent_l = []
    for step in range(1, SIDE):
        sent_l.append(copies.start(l0.at[0, (x + step) % SIDE], l1.at[0, step - 1], along_x[step - 1]))
        sent_l.append(copies.start(l0.at[1, :, (y + step) % SIDE], l1.at[1, step - 1], along_y[step - 1]))
    sent_g = [
        copies.start(gb.at[(dp + step) % GROUP], gbr.at[step - 1], peer) for step, peer in enumerate(peers, 1)
    ]
    again_in = reduce_second(1, found_in)
    home_out = send_home(0, reduce_last(0, again_out))
    wait_for(sent_l)
    for path in range(2):
        own_part = l0[0, x] if path == 0 else l0[1, :, y]
        l2[path] = (
            own_part.astype(f32) + l1[path, 0].astype(f32) + l1[path, 1].astype(f32) + l1[path, 2].astype(f32)
        ).astype(bf16)
    sent_l = []
    for step in range(1, SIDE):
        sent_l.append(copies.start(l2.at[0, (y + step) % SIDE], l3.at[0, step - 1], along_y[step - 1]))
        sent_l.append(copies.start(l2.at[1, (x + step) % SIDE], l3.at[1, step - 1], along_x[step - 1]))
    home_in = send_home(1, reduce_last(1, again_in))
    wait_for(sent_g)
    total = gb[dp]
    for step in range(GROUP - 1):
        total = total + gbr[step]
    gb1[...] = total
    gb2[2 * inner + c] = total
    sent_g = [copies.start(gb1, gb2.at[2 * inner + c], device) for device in octet]
    wait_for(sent_l)
    for path in range(2):
        own_part = l2[path, y if path == 0 else x]
        total = (own_part.astype(f32) + l3[path, 0].astype(f32)) + (l3[path, 1].astype(f32) + l3[path, 2].astype(f32))
        l4[2 * path] = total[0:16].astype(bf16)
        l4[2 * path + 1] = total[16:32].astype(bf16)
    sent_l = [copies.start(l4.at[(inner + step) % 4], l5.at[step - 1], along_in[step - 1]) for step in range(1, 4)]
    wait_for(sent_g)
    total = gb2[0]
    for i in range(1, 8):
        total = total + gb2[i]
    gb3[outer] = total
    sent_g = [copies.start(gb3.at[outer], gb3.at[outer], device) for device in along_out]
    wait_for(sent_l)
    l6[...] = (
        (l4[inner].astype(f32) + l5[0].astype(f32)) + (l5[1].astype(f32) + l5[2].astype(f32))
    ).astype(bf16)
    sent_l = [copies.start(l6, l7.at[outer], device) for device in along_out]
    l7[outer] = l6[...]

    wait_for(sent_l)
    fin[c, inner] = (
        (l7[0].astype(f32) + l7[1].astype(f32)) + (l7[2].astype(f32) + l7[3].astype(f32))
    ).astype(bf16)
    sent_l = [copies.start(fin.at[c, inner], fin.at[c, inner], device) for device in octet]
    wait_for(home_out)
    rows = returned(0)
    moe_out[...] = (
        gate_first * product(place_first, rows, 1, 0) + gate_second * product(place_second, rows, 1, 0)
    ).astype(bf16)
    wait_for(home_in)
    grad_norm = (product(place_all, returned(1), 1, 0) + base[...]) * gain_all
    mean_grad = jnp.mean(grad_norm, axis=1, keepdims=True)
    mean_both = jnp.mean(grad_norm * normed[...], axis=1, keepdims=True)
    grad_in[...] = (scale_inv * (grad_norm - mean_grad - normed[...] * mean_both)).astype(bf16)
    got_gd.wait_recv()
    gd_out[...] = (gd_own[...] + gdr[...].astype(f32)).astype(bf16)
    got_gu.wait_recv()
    gu_out[...] = (gu_own[...] + gur[...].astype(f32)).astype(bf16)
    wait_for(sent_g)
    total = (gb3[0] + gb3[1]) + (gb3[2] + gb3[3])
    gain_out[...] = total[0:1]
    bias_out[...] = total[1:2]
    wait_for(sent_l)
    router_out[...] = fin[...].astype(f32).reshape(128, 128)
    copies.finish()


def last_kernel(*refs):
    count = len(refs) // 2
    for i in range(count):
        refs[count + i][...] = refs[i][...]


def on_device(tokens, cotangent, routes, ln_gain, ln_bias, router_weight, up_weight, down_weight):
    vmem = pl.BlockSpec(memory_space=pltpu.VMEM)
    pair = (2, 2, CHUNK, UNITS)
    moved = (2, 2, SIDE, SIDE, ROWS, WIDTH)
    dense = (8, LANES)
    scratch = [
        ((TOKENS, HIDDEN), f32),
        ((2, 80, LANES), bf16),
        ((2, GROUP, 80, LANES), bf16),
        ((HIDDEN, LANES), bf16),
        ((2, GROUP, 16, LANES), bf16),
        ((2, GROUP, 16, LANES), bf16),
        (moved, bf16),
        ((WIDTH, UNITS), bf16),
        ((UNITS, WIDTH), bf16),
        (pair, f32),
        (pair, bf16),
        (pair, bf16),
        (pair, bf16),
        (pair, bf16),
        ((SIDE, CHUNK, UNITS), bf16),
        ((SIDE, CHUNK, UNITS), bf16),
        ((2, CHUNK, UNITS), f32),
        (moved, bf16),
        ((2, 2, SIDE - 1, SIDE, ROWS, WIDTH), bf16),
        ((2, 2, SIDE, ROWS, WIDTH), bf16),
        ((2, 2, SIDE - 1, ROWS, WIDTH), bf16),
        ((2, GROUP, 16, LANES), bf16),
        ((2, GROUP, 16, LANES), bf16),
        ((UNITS, WIDTH), bf16),
        ((UNITS, WIDTH), bf16),
        ((WIDTH, UNITS), bf16),
        ((WIDTH, UNITS), bf16),
        ((UNITS, WIDTH), f32),
        ((WIDTH, UNITS), f32),
        ((TOKENS, HIDDEN), f32),
        ((2, 2, SIDE, SIDE, 32, LANES), bf16),
        ((2, SIDE, SIDE, 32, LANES), bf16),
        ((2, SIDE, SIDE, 32, LANES), bf16),
        ((2, SIDE - 1, SIDE, 32, LANES), bf16),
        ((2, SIDE, 32, LANES), bf16),
        ((2, SIDE - 1, 32, LANES), bf16),
        ((4, 16, LANES), bf16),
        ((3, 16, LANES), bf16),
        ((16, LANES), bf16),
        ((4, 16, LANES), bf16),
        ((2, 4, 16, LANES), bf16),
        ((2, SIDE, CHUNK, WIDTH), bf16),
        ((GROUP,) + dense, f32),
        ((GROUP - 1,) + dense, f32),
        (dense, f32),
        ((8,) + dense, f32),
        ((4,) + dense, f32),
        ((GROUP,) + dense, f32),
        ((GROUP - 1,) + dense, f32),
        (dense, f32),
        ((GROUP,) + dense, f32),
    ]
    count = 256
    found = pl.pallas_call(
        step_kernel,
        out_shape=[
            jax.ShapeDtypeStruct(tokens.shape, bf16),
            jax.ShapeDtypeStruct(tokens.shape, bf16),
            jax.ShapeDtypeStruct((WIDTH, UNITS), bf16),
            jax.ShapeDtypeStruct((UNITS, WIDTH), bf16),
            jax.ShapeDtypeStruct((128, LANES), f32),
            jax.ShapeDtypeStruct((1, LANES), f32),
            jax.ShapeDtypeStruct((1, LANES), f32),
        ],
        in_specs=[vmem] * 8,
        out_specs=[vmem] * 7,
        scratch_shapes=[pltpu.VMEM(shape, kind) for shape, kind in scratch]
        + [pltpu.SemaphoreType.DMA((count,)), pltpu.SemaphoreType.DMA((count,))],
        compiler_params=pltpu.CompilerParams(collective_id=0, has_side_effects=True, vmem_limit_bytes=56 << 20),
    )(tokens, cotangent, routes.T, ln_gain[None], ln_bias[None], router_weight, up_weight[0], down_weight[0])
    moe_out, grad_input, grad_up, grad_down, grad_router, grad_gain, grad_bias = pl.pallas_call(
        last_kernel,
        out_shape=[jax.ShapeDtypeStruct(array.shape, array.dtype) for array in found],
        in_specs=[vmem] * 7,
        out_specs=[vmem] * 7,
        compiler_params=pltpu.CompilerParams(vmem_limit_bytes=60 << 20),
    )(*found)
    return (moe_out, grad_input, grad_up[None], grad_down[None], grad_router, grad_gain[0], grad_bias[0])


def solution(mesh):
    return jax.shard_map(
        on_device,
        mesh=mesh,
        in_specs=(
            P(("dp", "expert"), None),
            P(("dp", "expert"), None),
            P(("dp", "expert"), None),
            P("dp"),
            P("dp"),
            P("dp", None),
            P("expert", None, "dp"),
            P("expert", "dp", None),
        ),
        out_specs=(
            P(("dp", "expert"), None),
            P(("dp", "expert"), None),
            P("expert", None, "dp"),
            P("expert", "dp", None),
            P("dp", None),
            P("dp"),
            P("dp"),
        ),
        check_vma=False,
    )
```
